32 devices in a mesh: gx: 4 (over y, x), gy: 2 (over core), gz: 4 (over z).
Axes of the slice: x: 2, y: 2, z: 4, core: 2. Of those that a mesh axis runs over, the one named last changes fastest.
Arguments:
- field: float32 [4, 2048, 512], P(None, ('gx', 'gy', 'gz')), may hold values from -6 to 6
- neighbours: int32 [2048, 6], P(('gx', 'gy', 'gz')), may hold values from -1 to 2047, as said below
- cell_one: int32 [65536], P(('gx', 'gy', 'gz')), may hold values from 0 to 2047, as said below
- ref_one: float32 [3, 65536], P(None, ('gx', 'gy', 'gz')), may hold values from -1 to 1
- cell_two: int32 [65536], P(('gx', 'gy', 'gz')), may hold values from 0 to 2047, as said below
- ref_two: float32 [3, 65536], P(None, ('gx', 'gy', 'gz')), may hold values from -1 to 1
- velocity: float32 [3, 65536], P(None, ('gx', 'gy', 'gz')), may hold values from -6 to 6
- rate: float32 [65536], P(('gx', 'gy', 'gz')), may hold values from 0.5 to 8
- cut: int32 [1], replicated, may hold values from 1 to 2047
Outputs:
- field_out: float32 [4, 2048, 512], P(None, ('gx', 'gy', 'gz'))
- velocity_out: float32 [3, 65536], P(None, ('gx', 'gy', 'gz'))
The draws below stay inside these ranges and needn't reach their ends.
Inputs may be any that keep to these rules, and one draw needn't show every extreme that they name: `neighbours`: across face f of an element lies an element of the same device or of the adjacent device along that face's axis (cyclic along gz), with the same face node order; -1 marks walls at the ends along gx and gy. The order of elements within a device is arbitrary. `cell_one`: A particle's element is owned by a device with the same gx index as its bin. From one bin at most 512 particles lie in the elements of one device, and in each slab one device receives exactly 512 from every bin of the slab. `cell_two`: as for cell_one, for the second step's bins.
All inputs are finite; a program needn't handle non-finite values.
Results may differ from the reference program's by a relative error of at most 0.0003.
Values sent between devices are 32-bit elements; how exact they have to be, the bound alone decides.
A program may use at most 128 MiB of HBM per device.

```python
import math
import jax
import jax.numpy as jnp
import numpy as np
from jax import lax

NODES = 8
EDGE = 4
BIN = 2048
ELEMS = 2048
PARTICLES = 65536
N_GX = 4
N_GY = 2
N_GZ = 4
DEVICES = 32


def draw_neighbours(key, part):
    elements = EDGE * EDGE * EDGE
    orders = jax.vmap(lambda item_key: jax.random.permutation(item_key, elements))(jax.random.split(jax.random.fold_in(key, 5), DEVICES)).astype(jnp.int32)
    slot_at = jnp.argsort(orders, axis=1).astype(jnp.int32)
    device = jnp.arange(DEVICES, dtype=jnp.int32)[:, None]
    block_x = device // (N_GY * N_GZ)
    block_y = device // N_GZ % N_GY
    block_z = device % N_GZ
    coord_x = block_x * EDGE + orders // (EDGE * EDGE)
    coord_y = block_y * EDGE + orders // EDGE % EDGE
    coord_z = block_z * EDGE + orders % EDGE
    spans = (N_GX * EDGE, N_GY * EDGE, N_GZ * EDGE)
    columns = []
    for axis_index in range(3):
        for step_sign in (-1, 1):
            moved = [coord_x, coord_y, coord_z]
            shifted = moved[axis_index] + step_sign
            if axis_index == 2:
                inside = shifted == shifted
                shifted = shifted % spans[2]
            else:
                inside = (shifted >= 0) & (shifted < spans[axis_index])
                shifted = jnp.clip(shifted, 0, spans[axis_index] - 1)
            moved[axis_index] = shifted
            target_device = (moved[0] // EDGE * N_GY + moved[1] // EDGE) * N_GZ + moved[2] // EDGE
            target_position = (moved[0] % EDGE * EDGE + moved[1] % EDGE) * EDGE + moved[2] % EDGE
            target_slot = slot_at[target_device, target_position]
            columns.append(jnp.where(inside, target_device * elements + target_slot, -1))
    return jnp.stack(columns, axis=-1).reshape(DEVICES * elements, 6).astype(jnp.int32)


def particle_cells(key):
    owners = N_GY * N_GZ
    mean = BIN // owners
    capacity = 2 * mean
    elements = EDGE * EDGE * EDGE
    pattern = np.array([capacity] * (owners // 4) + [3 * mean // 4] * (owners // 2) + [mean // 2] * (owners // 4))
    bounds = jnp.asarray(np.cumsum(pattern), jnp.int32)
    special_key, bin_key = jax.random.split(key)
    special = jax.random.randint(special_key, (N_GX,), 0, owners).astype(jnp.int32)

    def one_bin(item_key, device):
        first_key, second_key, third_key = jax.random.split(item_key, 3)
        others = jax.random.permutation(first_key, owners - 1).astype(jnp.int32)
        slab = device // owners
        leader = special[slab]
        entry_owner = jnp.concatenate([leader[None], (leader + 1 + others) % owners])
        shuffled = jax.random.permutation(second_key, BIN).astype(jnp.int32)
        entry = jnp.searchsorted(bounds, shuffled, side='right').astype(jnp.int32)
        owner = entry_owner[entry]
        element = jax.random.randint(third_key, (BIN,), 0, elements).astype(jnp.int32)
        return (slab * owners + owner) * elements + element
    cells = jax.vmap(one_bin)(jax.random.split(bin_key, DEVICES), jnp.arange(DEVICES, dtype=jnp.int32))
    return cells.reshape(-1).astype(jnp.int32)


def draw_cell_one(key, part):
    return particle_cells(jax.random.fold_in(key, 11))


def draw_cell_two(key, part):
    return particle_cells(jax.random.fold_in(key, 23))


def levels(own_key, dims, cuts, smallest, high):
    loudness, own = 1.0, jax.random.fold_in(own_key, 6)
    for dim, blocks in cuts:
        heights = jnp.exp(jax.random.uniform(jax.random.fold_in(own, dim), (blocks,), jnp.float32, smallest / len(cuts), high / len(cuts)))
        loudness = loudness * jnp.repeat(heights, dims[dim] // blocks).reshape([-1 if axis == dim else 1 for axis in range(len(dims))])
    return loudness


def centred(stream_key, shape, width, bound, pieces=(), kind=jnp.bfloat16):
    values = jax.random.normal(stream_key, shape, jnp.float32) * width
    if len(pieces) > 0:
        values = levels(stream_key, shape, pieces, -0.22, 0.18) * values
    return jnp.clip(values, min=-bound, max=bound).astype(kind)


def setup_inputs(seed: int = 0) -> dict:
    streams_of = jax.random.split(jax.random.key(seed), 10)
    field = centred(streams_of[0], (4, ELEMS, NODES * NODES * NODES), 1.0, 6.0, ((1, 32),), jnp.float32)
    neighbours = draw_neighbours(jax.random.fold_in(streams_of[9], 71), 0)
    cell_one = draw_cell_one(jax.random.fold_in(streams_of[9], 71), 0)
    ref_one = jnp.clip(jax.random.uniform(streams_of[3], (3, PARTICLES), jnp.float32, -1.0, 1.0) * levels(streams_of[3], (3, PARTICLES), ((1, 32),), -0.4, 0.0), -1.0, 1.0)
    cell_two = draw_cell_two(jax.random.fold_in(streams_of[9], 71), 0)
    ref_two = jnp.clip(jax.random.uniform(streams_of[5], (3, PARTICLES), jnp.float32, -1.0, 1.0) * levels(streams_of[5], (3, PARTICLES), ((1, 32),), -0.4, 0.0), -1.0, 1.0)
    velocity = centred(streams_of[6], (3, PARTICLES), 1.0, 6.0, ((1, 32),), jnp.float32)
    rate = jnp.clip(jnp.exp(math.log(8.0) - 2.7725887 * jax.random.uniform(streams_of[7], (PARTICLES,), jnp.float32) ** levels(streams_of[7], (PARTICLES,), ((0, 32),), -0.2, 0.2)), 0.5, 8.0)
    cut = jax.random.randint(streams_of[8], (1,), 1, BIN).astype(jnp.int32)
    return dict(field=field, neighbours=neighbours, cell_one=cell_one, ref_one=ref_one, cell_two=cell_two, ref_two=ref_two, velocity=velocity, rate=rate, cut=cut)


node_points = -np.cos(np.pi * np.arange(8) / 7.0)
step_time = 0.1
viscosity = 0.002
penalty = 0.25
loading = 0.5
heating = 0.5


def gap_table():
    differences = node_points[:, None] - node_points[None, :] + np.eye(8)
    inverse = 1.0 / differences
    return inverse * (1.0 - np.eye(8))


def laplace_table():
    differences = node_points[:, None] - node_points[None, :] + np.eye(8)
    weights = 1.0 / np.prod(differences, axis=1)
    derivative = (weights[None, :] / weights[:, None]) / differences
    derivative = derivative * (1.0 - np.eye(8))
    derivative = derivative - np.eye(8) * derivative.sum(axis=1)[:, None]
    second = derivative @ derivative
    identity = np.eye(8)
    operator = np.kron(np.kron(second, identity), identity)
    operator = operator + np.kron(np.kron(identity, second), identity)
    operator = operator + np.kron(np.kron(identity, identity), second)
    return operator.T


def face_table():
    selection = np.zeros((512, 384))
    for face_side in range(6):
        edge_value = 0 if face_side % 2 == 0 else 7
        for row_node in range(8):
            for col_node in range(8):
                if face_side < 2:
                    node_index = (edge_value * 8 + row_node) * 8 + col_node
                elif face_side < 4:
                    node_index = (row_node * 8 + edge_value) * 8 + col_node
                else:
                    node_index = (row_node * 8 + col_node) * 8 + edge_value
                selection[node_index, face_side * 64 + row_node * 8 + col_node] = 1.0
    return selection


def expand_table(direction):
    positions = np.arange(512)
    digits = (positions // (8 ** (2 - direction))) % 8
    return np.where(digits[None, :] == np.arange(8)[:, None], 1.0, 0.0)


def lagrange(coordinate):
    points = jnp.asarray(node_points, jnp.float32)
    inverse = jnp.asarray(gap_table(), jnp.float32)
    identity = jnp.eye(8, dtype=jnp.float32)
    offsets = coordinate[:, None] - points[None, :]
    factors = offsets[:, None, :] * inverse[None, :, :] + identity[None, :, :]
    return jnp.prod(factors, axis=2)


def basis(coords):
    result = None
    for direction in range(3):
        spread = jnp.dot(lagrange(coords[direction]), jnp.asarray(expand_table(direction), jnp.float32), precision=lax.Precision.HIGHEST)
        result = spread if result is None else result * spread
    return result


def surface_jump(field, neighbours):
    selection = jnp.asarray(face_table(), jnp.float32)
    elements = field.shape[1]
    faces = jnp.dot(field.reshape(-1, 512), selection, precision=lax.Precision.HIGHEST).reshape(4, elements, 6, 64)
    jumps = []
    for face_side in range(6):
        target = neighbours[:, face_side]
        present = target >= 0
        partner = faces[:, jnp.maximum(target, 0), face_side ^ 1, :]
        partner = jnp.where(present[None, :, None], partner, jnp.zeros_like(partner))
        jumps.append(partner - faces[:, :, face_side, :])
    joined = jnp.stack(jumps, axis=2).reshape(-1, 384)
    return jnp.dot(joined, selection.T, precision=lax.Precision.HIGHEST).reshape(field.shape)


def fluid_step(field, neighbours, force):
    laplace = jnp.dot(field.reshape(-1, 512), jnp.asarray(laplace_table(), jnp.float32), precision=lax.Precision.HIGHEST).reshape(field.shape)
    coupling = jnp.asarray([-loading, -loading, -loading, heating], jnp.float32)
    return field + viscosity * laplace + penalty * surface_jump(field, neighbours) + coupling[:, None, None] * force


def coupled_step(field, neighbours, cells, coords, speeds, rates):
    total = cells.shape[0]
    block_size = 8192
    blocks = total // block_size
    cell_blocks = cells.reshape(blocks, block_size)
    coord_blocks = coords.reshape(3, blocks, block_size).transpose(1, 0, 2)
    speed_blocks = speeds.reshape(3, blocks, block_size).transpose(1, 0, 2)
    rate_blocks = rates.reshape(blocks, block_size)

    def visit(force, inputs):
        cell_block, coord_block, speed_block, rate_block = inputs
        weights = basis(coord_block)
        gathered = field[:3, cell_block, :]
        fluid = jnp.sum(gathered * weights[None], axis=2)
        offset_block = fluid - speed_block
        accel = rate_block[None] * offset_block
        heat = rate_block * jnp.sum(offset_block * offset_block, axis=0)
        fresh = speed_block + step_time * accel
        sources = jnp.concatenate([accel, heat[None]], axis=0)
        force = force.at[:, cell_block, :].add(sources[:, :, None] * weights[None])
        return force, fresh

    force, fresh = lax.scan(visit, jnp.zeros(field.shape, jnp.float32), (cell_blocks, coord_blocks, speed_blocks, rate_blocks))
    new_speeds = fresh.transpose(1, 0, 2).reshape(3, total)
    return fluid_step(field, neighbours, force), new_speeds


def migrate(values, cut):
    rows = values.shape[0]
    slab = N_GY * N_GZ * BIN
    grouped = values.reshape(rows, N_GX, slab)
    doubled = jnp.concatenate([grouped, grouped], axis=2)
    moved = lax.dynamic_slice_in_dim(doubled, cut[0].astype(jnp.int32), slab, 2)
    return moved.reshape(rows, -1)


def reference(field, neighbours, cell_one, ref_one, cell_two, ref_two, velocity, rate, cut):
    middle, speeds = coupled_step(field, neighbours, cell_one, ref_one, velocity, rate)
    carried = migrate(jnp.concatenate([speeds, rate[None]], axis=0), cut)
    final, speeds_two = coupled_step(middle, neighbours, cell_two, ref_two, carried[:3], carried[3])
    return final, speeds_two
```

```python
import functools
import jax
import jax.numpy as jnp
import numpy as np
from jax import lax
from jax.experimental import pallas as pl
from jax.experimental.pallas import tpu as pltpu
from jax.sharding import PartitionSpec as P

EDGE = 4
node_points = -np.cos(np.pi * np.arange(8) / 7.0)
step_time = 0.1
viscosity = 0.002
penalty = 0.25
couplings = (-0.5, -0.5, -0.5, 0.5)
f32 = jnp.float32
b16 = jnp.bfloat16
MESH = pl.DeviceIdType.MESH


def gap_table():
    differences = node_points[:, None] - node_points[None, :] + np.eye(8)
    inverse = 1.0 / differences
    return inverse * (1.0 - np.eye(8))


def laplace_table():
    differences = node_points[:, None] - node_points[None, :] + np.eye(8)
    weights = 1.0 / np.prod(differences, axis=1)
    derivative = weights[None, :] / weights[:, None] / differences
    derivative = derivative * (1.0 - np.eye(8))
    derivative = derivative - np.eye(8) * derivative.sum(axis=1)[:, None]
    second = derivative @ derivative
    identity = np.eye(8)
    operator = np.kron(np.kron(second, identity), identity)
    operator = operator + np.kron(np.kron(identity, second), identity)
    operator = operator + np.kron(np.kron(identity, identity), second)
    return operator.T


def face_table():
    selection = np.zeros((512, 384))
    for side in range(6):
        edge = 0 if side % 2 == 0 else 7
        for row in range(8):
            for col in range(8):
                if side < 2:
                    node = (edge * 8 + row) * 8 + col
                elif side < 4:
                    node = (row * 8 + edge) * 8 + col
                else:
                    node = (row * 8 + col) * 8 + edge
                selection[node, side * 64 + row * 8 + col] = 1.0
    return selection


def mm(a, b):
    return lax.dot_general(a, b, (((1,), (0,)), ((), ())), preferred_element_type=f32)


def nt(a, b):
    return lax.dot_general(a, b, (((1,), (1,)), ((), ())), preferred_element_type=f32)


def split2(x):
    hi = x.astype(b16)
    return hi, (x - hi.astype(f32)).astype(b16)


def split3(x):
    hi = x.astype(b16)
    rest = x - hi.astype(f32)
    mid = rest.astype(b16)
    return hi, mid, (rest - mid.astype(f32)).astype(b16)


def iota(shape, dim):
    return lax.broadcasted_iota(jnp.int32, shape, dim)


def fiota(shape, dim):
    return iota(shape, dim).astype(f32)


def quotient(x, n):
    return jnp.floor((x + 0.5) * (1.0 / n))


def onehot(mask):
    return jnp.where(mask, 1.0, 0.0).astype(f32)


class Sizes:
    def __init__(self, owners, elements, particles):
        self.owners, self.elements, self.particles = owners, elements, particles
        self.cap = 2 * particles // owners
        self.lw = min(128, self.cap)
        self.bpo = self.cap // self.lw
        self.tiles = owners * self.bpo
        self.rpb = -(-3 * self.bpo // 8) * 8
        self.opc = max(1, 512 // self.cap)
        self.chunk = self.opc * self.cap
        self.tpc = self.opc * self.bpo
        self.chunks = owners // self.opc
        self.edge = EDGE * EDGE


def place(z, cell):
    number = cell.astype(f32)
    device = quotient(number, z.elements)
    element = number - device * z.elements
    owner = device - quotient(device, z.owners) * z.owners
    marks = onehot(fiota((z.owners, z.particles), 0) == owner)
    parts = z.particles // 128
    rows = parts * z.owners
    stacked = jnp.concatenate([marks[:, c * 128 : (c + 1) * 128] for c in range(parts)], axis=0)
    upper = onehot(iota((128, 128), 0) <= iota((128, 128), 1)).astype(b16)
    inside = mm(stacked.astype(b16), upper)
    totals = jnp.broadcast_to(inside[:, 127:128], (rows, 128)).astype(b16)
    row, col = fiota((rows, rows), 0), fiota((rows, rows), 1)
    row_part, col_part = quotient(row, z.owners), quotient(col, z.owners)
    same = (row - row_part * z.owners) == (col - col_part * z.owners)
    earlier = onehot(same & (col_part < row_part)).astype(b16)
    owner_of = fiota((rows, 128), 0)
    owner_of = owner_of - quotient(owner_of, z.owners) * z.owners
    value = stacked * (inside - 1.0 + mm(earlier, totals) + owner_of * z.cap)
    slot = jnp.concatenate(
        [
            jnp.sum(value[c * z.owners : (c + 1) * z.owners], axis=0, keepdims=True)
            for c in range(parts)
        ],
        axis=1,
    )
    return element, slot


def slot_parts(z, slot):
    high = quotient(slot, z.lw)
    low = slot - high * z.lw
    return high, onehot(fiota((z.lw, z.particles), 0) == low).astype(b16)


def pack(z, payload, slot):
    high, low = slot_parts(z, slot)
    three = jnp.concatenate([part.astype(f32) for part in split3(payload)], axis=0)
    spread = jnp.concatenate(
        [jnp.where(high == float(i), three, 0.0).astype(b16) for i in range(z.tiles)], axis=0
    )
    moved = nt(spread, low).reshape(z.tiles, 3, 8, z.lw)
    return moved[:, 0] + moved[:, 1] + moved[:, 2]


def unpack(z, block, slot):
    high, low = slot_parts(z, slot)
    rows = z.owners * z.rpb
    flat = block.reshape(rows, z.lw)
    got = mm(jnp.concatenate(split3(flat), axis=0), low)
    got = got[:rows] + got[rows : 2 * rows] + got[2 * rows :]
    row = fiota((z.rpb, z.particles), 0)
    key = high - (row - quotient(row, z.bpo) * z.bpo)
    total = jnp.zeros((z.rpb, z.particles), f32)
    for o in range(z.owners):
        total = total + jnp.where(
            key == float(o * z.bpo), got[o * z.rpb : (o + 1) * z.rpb], 0.0
        )
    return jnp.concatenate(
        [
            jnp.sum(total[v * z.bpo : (v + 1) * z.bpo], axis=0, keepdims=True)
            for v in range(3)
        ],
        axis=0,
    )


def lagrange(x, table):
    result = None
    for m in range(8):
        factor = (x - float(np.float32(node_points[m]))) * table[:, m : m + 1]
        factor = factor + table[:, 8 + m : 9 + m]
        result = factor if result is None else result * factor
    return result


def basis(coords, table):
    first, second, third = [lagrange(coords[d : d + 1], table) for d in range(3)]
    plane = jnp.concatenate([second[b : b + 1] * third for b in range(8)], axis=0)
    return jnp.concatenate([first[a : a + 1] * plane for a in range(8)], axis=0)


def kernel(
    z, axes, field_ref, nbr_ref, nbr_t_ref, cell_one_ref, ref_one_ref, cell_two_ref, ref_two_ref,
    vel_ref, rate_ref, cut_ref, own_hi_ref, own_lo_ref, sel_ref, sel_t_ref, table_ref,
    field_out_ref, vel_out_ref,
    out_buf, in_buf, ret_out, ret_in, carry_out, carry_in, face_out, face_in,
    w_hi, w_lo, src, force_ref, mid_ref,
    a2a_send, a2a_recv, ret_send, ret_recv, face_send, face_recv, carry_sems,
):
    count_x, count_y, count_z = axes
    ix, iy, iz = lax.axis_index("gx"), lax.axis_index("gy"), lax.axis_index("gz")
    me = iy * count_z + iz
    elements, n_own = z.elements, z.owners
    base = ((ix * n_own + me) * elements).astype(jnp.int32)

    def member(index):
        return (ix, index // count_z, index % count_z)

    def peer(r):
        return lax.rem(me + r, n_own)

    barrier = pltpu.get_barrier_semaphore()

    def greet(r, _):
        pl.semaphore_signal(barrier, inc=1, device_id=member(peer(r)), device_id_type=MESH)
        return 0

    lax.fori_loop(1, n_own, greet, 0)
    up_x = (lax.rem(ix + 1, count_x), iy, iz)
    down_x = (lax.rem(ix + count_x - 1, count_x), iy, iz)
    for device in (up_x, down_x):
        pl.semaphore_signal(barrier, inc=1, device_id=device, device_id_type=MESH)

    def part_copy(stage, r):
        to = peer(r)
        return pltpu.make_async_remote_copy(
            src_ref=out_buf.at[stage, pl.ds(to * z.bpo, z.bpo)],
            dst_ref=in_buf.at[stage, pl.ds(me * z.bpo, z.bpo)],
            send_sem=a2a_send.at[stage, r],
            recv_sem=a2a_recv.at[stage, r],
            device_id=member(to),
            device_id_type=MESH,
        )

    def ret_copy(stage, r):
        to = peer(r)
        return pltpu.make_async_remote_copy(
            src_ref=ret_out.at[stage, to],
            dst_ref=ret_in.at[stage, me],
            send_sem=ret_send.at[stage, r],
            recv_sem=ret_recv.at[stage, r],
            device_id=member(to),
            device_id_type=MESH,
        )

    def start_all(make, stage):
        def body(r, _):
            make(stage, r).start()
            return 0

        lax.fori_loop(1, n_own, body, 0)

    def wait_all(make, stage):
        def body(r, _):
            make(stage, r).wait()
            return 0

        lax.fori_loop(1, n_own, body, 0)

    def send_parts(stage, packed):
        out_buf[stage] = packed
        own = pl.ds(me * z.bpo, z.bpo)
        in_buf[stage, own] = out_buf[stage, own]
        start_all(part_copy, stage)

    def send_back(stage):
        ret_in[stage, me] = ret_out[stage, me]
        start_all(ret_copy, stage)

    face_devices = [
        down_x,
        up_x,
        (ix, lax.rem(iy + count_y - 1, count_y), iz),
        (ix, lax.rem(iy + 1, count_y), iz),
        (ix, iy, lax.rem(iz + count_z - 1, count_z)),
        (ix, iy, lax.rem(iz + 1, count_z)),
    ]

    def face_copy(stage, side):
        return pltpu.make_async_remote_copy(
            src_ref=face_out.at[stage, side],
            dst_ref=face_in.at[stage, side ^ 1],
            send_sem=face_send.at[stage, side],
            recv_sem=face_recv.at[stage, side ^ 1],
            device_id=face_devices[side],
            device_id_type=MESH,
        )

    def face_wait(stage):
        for side in range(6):
            face_copy(stage, side).wait_send()
        for side in range(6):
            pltpu.make_async_remote_copy(
                src_ref=face_out.at[stage, side ^ 1],
                dst_ref=face_in.at[stage, side],
                send_sem=face_send.at[stage, side ^ 1],
                recv_sem=face_recv.at[stage, side],
                device_id=face_devices[side],
                device_id_type=MESH,
            ).wait_recv()

    table = table_ref[...]

    rate = rate_ref[...]
    element, slot_one = place(z, cell_one_ref[...])
    packed = pack(
        z, jnp.concatenate([element + 1.0, ref_one_ref[...], vel_ref[...], rate], axis=0), slot_one
    )
    pl.semaphore_wait(barrier, n_own - 1 + 2)
    send_parts(0, packed)

    square = (elements, elements)
    compacts, partners = [], []
    for side in range(6):
        col = nbr_ref[:, side : side + 1]
        row = nbr_t_ref[side : side + 1, :]
        col_out = (col < base) | (col >= base + elements)
        row_out = (row < base) | (row >= base + elements)
        before = jnp.where(col_out & (iota(square, 0) < iota(square, 1)), 1.0, 0.0)
        before = jnp.sum(before, axis=0, keepdims=True)
        compact = onehot((fiota((z.edge, elements), 0) == before) & row_out).astype(b16)
        compacts.append(jnp.concatenate([compact, compact], axis=1))
        here = onehot(iota(square, 1) == col - base).astype(b16)
        lower = jnp.where(row_out & (row >= 0) & (row < col), 1.0, 0.0)
        rank = jnp.sum(lower, axis=1, keepdims=True)
        far = onehot((fiota((elements, z.edge), 1) == rank) & col_out & (col >= 0)).astype(b16)
        partners.append(jnp.concatenate([here, here, far, far], axis=1))

    def split_state(state):
        return split2(state.reshape(4 * elements, 512))

    def send_faces(stage, hi, lo):
        both = mm(jnp.concatenate([hi, lo], axis=0), sel_ref[...])
        faces = both[: 4 * elements] + both[4 * elements :]
        wide = []
        for side in range(6):
            lanes = jnp.concatenate(
                [
                    faces[k * elements : (k + 1) * elements, side * 64 : (side + 1) * 64]
                    for k in range(4)
                ],
                axis=1,
            )
            pair = jnp.concatenate(split2(lanes), axis=0)
            wide.append(pair)
            face_out[stage, side] = mm(compacts[side], pair)
            face_copy(stage, side).start()
        return wide

    def own_part(state, hi, lo):
        both = mm(jnp.concatenate([hi, lo], axis=0), own_hi_ref[...])
        rows = 4 * elements
        return state + both[:rows] + both[rows:] + mm(hi, own_lo_ref[...])

    def partner_part(stage, wide):
        got = []
        for side in range(6):
            far = jnp.concatenate(split2(face_in[stage, side]), axis=0)
            got.append(mm(partners[side], jnp.concatenate([wide[side ^ 1], far], axis=0)))
        joined = jnp.concatenate(
            [
                jnp.concatenate([got[side][:, k * 64 : (k + 1) * 64] for side in range(6)], axis=1)
                for k in range(4)
            ],
            axis=0,
        )
        hi, lo = split2(joined)
        rows = 4 * elements
        both = mm(jnp.concatenate([hi, lo], axis=0), sel_t_ref[...])
        return penalty * (both[:rows] + both[rows:])

    def chunk_rows(stage, i):
        piece = in_buf[stage, pl.ds(i * z.tpc, z.tpc)]
        return jnp.concatenate([piece[t] for t in range(z.tpc)], axis=1)

    def build(stage, where, i):
        weights = basis(chunk_rows(stage, i)[1:4], table)
        hi, lo = split2(weights)
        w_hi[where, i] = hi
        w_lo[where, i] = lo

    def sample(stage_pos, stage_vel, where, hi, lo, i):
        rows = 3 * elements
        both = mm(jnp.concatenate([hi[:rows], lo[:rows]], axis=0), w_hi[where, i])
        values = both[:rows] + both[rows:] + mm(hi[:rows], w_lo[where, i])
        pos = chunk_rows(stage_pos, i)
        dyn = pos if stage_pos == stage_vel else chunk_rows(stage_vel, i)
        pick = fiota((elements, z.chunk), 0) == pos[0:1] - 1.0
        fluid = jnp.concatenate(
            [
                jnp.sum(
                    jnp.where(pick, values[k * elements : (k + 1) * elements], 0.0),
                    axis=0,
                    keepdims=True,
                )
                for k in range(3)
            ],
            axis=0,
        )
        speeds, rates = dyn[4:7], dyn[7:8]
        offset = fluid - speeds
        accel = rates * offset
        heat = rates * jnp.sum(offset * offset, axis=0, keepdims=True)
        fresh = speeds + step_time * accel
        src[where, i] = jnp.concatenate(
            [couplings[0] * accel, couplings[3] * heat, pos[0:1], fresh], axis=0
        )
        for j in range(z.opc):
            rows = []
            for v in range(3):
                for b in range(z.bpo):
                    at = j * z.cap + b * z.lw
                    rows.append(fresh[v : v + 1, at : at + z.lw])
            if z.rpb > 3 * z.bpo:
                rows.append(jnp.zeros((z.rpb - 3 * z.bpo, z.lw), f32))
            ret_out[where, i * z.opc + j] = jnp.concatenate(rows, axis=0)

    def spread(where, i):
        data = src[where, i]
        pick = fiota((elements, z.chunk), 0) == data[4:5] - 1.0
        loads = jnp.concatenate([jnp.where(pick, data[k : k + 1], 0.0) for k in range(4)], axis=0)
        hi, lo = split2(loads)
        both = nt(w_hi[where, i], jnp.concatenate([hi, lo], axis=0))
        rows = 4 * elements
        force_ref[...] += both[:, :rows] + both[:, rows:] + nt(w_lo[where, i], hi)

    def loop(body):
        def step(i, _):
            body(i)
            return 0

        lax.fori_loop(0, z.chunks, step, 0)

    def forces(where):
        force_ref[...] = jnp.zeros_like(force_ref)
        loop(functools.partial(spread, where))
        return force_ref[...].T

    state = field_ref[...].reshape(4 * elements, 512)
    hi, lo = split2(state)
    wide = send_faces(0, hi, lo)

    element, slot_two = place(z, cell_two_ref[...])
    blank = jnp.zeros((4, z.particles), f32)
    packed = pack(z, jnp.concatenate([element + 1.0, ref_two_ref[...], blank], axis=0), slot_two)
    send_parts(1, packed)

    wait_all(part_copy, 0)

    def first(i):
        build(0, 0, i)
        sample(0, 0, 0, hi, lo, i)

    loop(first)
    send_back(0)
    mid_ref[...] = own_part(state, hi, lo)
    mid_ref[...] += forces(0)
    wait_all(ret_copy, 0)
    carried = jnp.concatenate(
        [unpack(z, ret_in[0], slot_one), rate, jnp.zeros((4, z.particles), f32)], axis=0
    )
    carry_out[...] = carried
    carry = pltpu.make_async_remote_copy(
        src_ref=carry_out,
        dst_ref=carry_in,
        send_sem=carry_sems.at[0],
        recv_sem=carry_sems.at[1],
        device_id=member(lax.rem(me + n_own - 1, n_own)),
        device_id_type=MESH,
    )
    carry.start()
    face_wait(0)
    state = mid_ref[...] + partner_part(0, wide)
    hi, lo = split2(state)
    wide = send_faces(1, hi, lo)
    mid_ref[...] = own_part(state, hi, lo)
    wait_all(part_copy, 1)
    loop(functools.partial(build, 1, 1))
    carry.wait()
    moved = jnp.concatenate([carry_out[...], carry_in[...]], axis=1)
    cut = cut_ref[0]
    bit, width = 1, 2 * z.particles
    while bit < z.particles:
        flag = jnp.full((8, width), (cut // bit) % 2, jnp.int32)
        moved = jnp.where(flag == 1, pltpu.roll(moved, width - bit, 1), moved)
        bit *= 2
    moved = moved[:, : z.particles]
    send_parts(2, pack(z, jnp.concatenate([blank, moved[:4]], axis=0), slot_two))
    wait_all(part_copy, 2)
    loop(functools.partial(sample, 1, 2, 1, hi, lo))
    send_back(1)
    mid_ref[...] += forces(1)
    face_wait(1)
    final = mid_ref[...] + partner_part(1, wide)
    field_out_ref[...] = final.reshape(4, elements, 512)
    wait_all(ret_copy, 1)
    vel_out_ref[...] = unpack(z, ret_in[1], slot_two)


def local(axes, field, neighbours, cell_one, ref_one, cell_two, ref_two, velocity, rate, cut):
    elements, particles = field.shape[1], cell_one.shape[0]
    owners = axes[1] * axes[2]
    z = Sizes(owners, elements, particles)
    selection = face_table()
    own = viscosity * laplace_table() - penalty * np.diag(selection.sum(axis=1))
    own_hi = own.astype(np.float32).astype(b16)
    own_lo = (own - own_hi.astype(np.float64)).astype(np.float32).astype(b16)
    table = np.concatenate([gap_table(), np.eye(8)], axis=1).astype(np.float32)
    vmem = pl.BlockSpec(memory_space=pltpu.VMEM)
    args = [
        field,
        neighbours,
        neighbours.T,
        cell_one[None],
        ref_one,
        cell_two[None],
        ref_two,
        velocity,
        rate[None],
        cut,
        jnp.asarray(own_hi),
        jnp.asarray(own_lo),
        jnp.asarray(selection, b16),
        jnp.asarray(selection.T, b16),
        jnp.asarray(table),
    ]
    specs = [vmem] * len(args)
    specs[9] = pl.BlockSpec(memory_space=pltpu.SMEM)
    dma = pltpu.SemaphoreType.DMA
    return pl.pallas_call(
        functools.partial(kernel, z, axes),
        out_shape=(
            jax.ShapeDtypeStruct(field.shape, f32),
            jax.ShapeDtypeStruct(velocity.shape, f32),
        ),
        in_specs=specs,
        out_specs=(vmem, vmem),
        scratch_shapes=[
            pltpu.VMEM((3, z.tiles, 8, z.lw), f32),
            pltpu.VMEM((3, z.tiles, 8, z.lw), f32),
            pltpu.VMEM((2, owners, z.rpb, z.lw), f32),
            pltpu.VMEM((2, owners, z.rpb, z.lw), f32),
            pltpu.VMEM((8, particles), f32),
            pltpu.VMEM((8, particles), f32),
            pltpu.VMEM((2, 6, z.edge, 256), f32),
            pltpu.VMEM((2, 6, z.edge, 256), f32),
            pltpu.VMEM((2, z.chunks, 512, z.chunk), b16),
            pltpu.VMEM((2, z.chunks, 512, z.chunk), b16),
            pltpu.VMEM((2, z.chunks, 8, z.chunk), f32),
            pltpu.VMEM((512, 4 * elements), f32),
            pltpu.VMEM((4 * elements, 512), f32),
            dma((3, owners)),
            dma((3, owners)),
            dma((2, owners)),
            dma((2, owners)),
            dma((2, 6)),
            dma((2, 6)),
            dma((2,)),
        ],
        compiler_params=pltpu.CompilerParams(
            collective_id=0, has_side_effects=True, vmem_limit_bytes=56 * 1024 * 1024
        ),
    )(*args)


def solution(mesh):
    axes = (mesh.shape["gx"], mesh.shape["gy"], mesh.shape["gz"])
    in_specs = (
        P(None, ("gx", "gy", "gz"), None),
        P(("gx", "gy", "gz"), None),
        P(("gx", "gy", "gz")),
        P(None, ("gx", "gy", "gz")),
        P(("gx", "gy", "gz")),
        P(None, ("gx", "gy", "gz")),
        P(None, ("gx", "gy", "gz")),
        P(("gx", "gy", "gz")),
        P(),
    )
    out_specs = (P(None, ("gx", "gy", "gz"), None), P(None, ("gx", "gy", "gz")))
    return jax.shard_map(
        functools.partial(local, axes), mesh=mesh, in_specs=in_specs, out_specs=out_specs,
        check_vma=False,
    )
```

```python
import functools
import jax
import jax.numpy as jnp
import numpy as np
from jax import lax
from jax.experimental import pallas as pl
from jax.experimental.pallas import tpu as pltpu
from jax.sharding import PartitionSpec as P

EDGE = 4
node_points = -np.cos(np.pi * np.arange(8) / 7.0)
step_time = 0.1
viscosity = 0.002
penalty = 0.25
couplings = (-0.5, -0.5, -0.5, 0.5)
f32 = jnp.float32
b16 = jnp.bfloat16
MESH = pl.DeviceIdType.MESH


def gap_table():
    differences = node_points[:, None] - node_points[None, :] + np.eye(8)
    inverse = 1.0 / differences
    return inverse * (1.0 - np.eye(8))


def laplace_table():
    differences = node_points[:, None] - node_points[None, :] + np.eye(8)
    weights = 1.0 / np.prod(differences, axis=1)
    derivative = weights[None, :] / weights[:, None] / differences
    derivative = derivative * (1.0 - np.eye(8))
    derivative = derivative - np.eye(8) * derivative.sum(axis=1)[:, None]
    second = derivative @ derivative
    identity = np.eye(8)
    operator = np.kron(np.kron(second, identity), identity)
    operator = operator + np.kron(np.kron(identity, second), identity)
    operator = operator + np.kron(np.kron(identity, identity), second)
    return operator.T


def face_table():
    selection = np.zeros((512, 384))
    for side in range(6):
        edge = 0 if side % 2 == 0 else 7
        for row in range(8):
            for col in range(8):
                if side < 2:
                    node = (edge * 8 + row) * 8 + col
                elif side < 4:
                    node = (row * 8 + edge) * 8 + col
                else:
                    node = (row * 8 + col) * 8 + edge
                selection[node, side * 64 + row * 8 + col] = 1.0
    return selection


def mm(a, b):
    return lax.dot_general(a, b, (((1,), (0,)), ((), ())), preferred_element_type=f32)


def nt(a, b):
    return lax.dot_general(a, b, (((1,), (1,)), ((), ())), preferred_element_type=f32)


def split2(x):
    hi = x.astype(b16)
    return hi, (x - hi.astype(f32)).astype(b16)


def split3(x):
    hi = x.astype(b16)
    rest = x - hi.astype(f32)
    mid = rest.astype(b16)
    return hi, mid, (rest - mid.astype(f32)).astype(b16)


def iota(shape, dim):
    return lax.broadcasted_iota(jnp.int32, shape, dim)


def fiota(shape, dim):
    return iota(shape, dim).astype(f32)


def quotient(x, n):
    return jnp.floor((x + 0.5) * (1.0 / n))


def onehot(mask):
    return jnp.where(mask, 1.0, 0.0).astype(f32)


class Sizes:
    def __init__(self, owners, elements, particles):
        self.owners, self.elements, self.particles = owners, elements, particles
        self.cap = 2 * particles // owners
        self.lw = min(128, self.cap)
        self.bpo = self.cap // self.lw
        self.tiles = owners * self.bpo
        self.rpb = -(-3 * self.bpo // 8) * 8
        self.opc = max(1, 512 // self.cap)
        self.chunk = self.opc * self.cap
        self.tpc = self.opc * self.bpo
        self.chunks = owners // self.opc
        self.edge = EDGE * EDGE


def place(z, cell):
    number = cell.astype(f32)
    device = quotient(number, z.elements)
    element = number - device * z.elements
    owner = device - quotient(device, z.owners) * z.owners
    marks = onehot(fiota((z.owners, z.particles), 0) == owner)
    parts = z.particles // 128
    rows = parts * z.owners
    stacked = jnp.concatenate([marks[:, c * 128 : (c + 1) * 128] for c in range(parts)], axis=0)
    upper = onehot(iota((128, 128), 0) <= iota((128, 128), 1)).astype(b16)
    inside = mm(stacked.astype(b16), upper)
    totals = jnp.broadcast_to(inside[:, 127:128], (rows, 128)).astype(b16)
    row, col = fiota((rows, rows), 0), fiota((rows, rows), 1)
    row_part, col_part = quotient(row, z.owners), quotient(col, z.owners)
    same = (row - row_part * z.owners) == (col - col_part * z.owners)
    earlier = onehot(same & (col_part < row_part)).astype(b16)
    owner_of = fiota((rows, 128), 0)
    owner_of = owner_of - quotient(owner_of, z.owners) * z.owners
    value = stacked * (inside - 1.0 + mm(earlier, totals) + owner_of * z.cap)
    slot = jnp.concatenate(
        [
            jnp.sum(value[c * z.owners : (c + 1) * z.owners], axis=0, keepdims=True)
            for c in range(parts)
        ],
        axis=1,
    )
    return element, slot


def slot_parts(z, slot):
    high = quotient(slot, z.lw)
    low = slot - high * z.lw
    return high, onehot(fiota((z.lw, z.particles), 0) == low).astype(b16)


def pack(z, payload, slot):
    fields = payload.shape[0]
    high, low = slot_parts(z, slot)
    two = jnp.concatenate([part.astype(f32) for part in split2(payload)], axis=0)
    spread = jnp.concatenate(
        [jnp.where(high == float(i), two, 0.0) for i in range(z.tiles)], axis=0
    ).astype(b16)
    moved = nt(spread, low).reshape(z.tiles, 2 * fields, z.lw)
    return moved[:, :fields] + moved[:, fields:]


def unpack(z, block, slot):
    high, low = slot_parts(z, slot)
    rows = z.owners * z.rpb
    flat = block.reshape(rows, z.lw)
    got = mm(jnp.concatenate(split2(flat), axis=0), low)
    got = got[:rows] + got[rows:]
    row = fiota((z.rpb, z.particles), 0)
    key = high - (row - quotient(row, z.bpo) * z.bpo)
    total = jnp.zeros((z.rpb, z.particles), f32)
    for o in range(z.owners):
        total = total + jnp.where(
            key == float(o * z.bpo), got[o * z.rpb : (o + 1) * z.rpb], 0.0
        )
    return jnp.concatenate(
        [
            jnp.sum(total[v * z.bpo : (v + 1) * z.bpo], axis=0, keepdims=True)
            for v in range(3)
        ],
        axis=0,
    )


def shift(z, pair, cut):
    bit = 1 << (z.particles - 1).bit_length() - 1
    while bit >= 1:
        flag = jnp.full(pair.shape, (cut // bit) % 2, jnp.int32) == 1
        if bit >= 128:
            width = z.particles + bit
            pair = jnp.where(flag[:, :width], pair[:, bit : bit + width], pair[:, :width])
        else:
            pair = jnp.where(flag, pltpu.roll(pair, pair.shape[1] - bit, 1), pair)
        bit //= 2
    return pair[:, : z.particles]


def lagrange(x, table):
    result = None
    for m in range(8):
        factor = (x - float(np.float32(node_points[m]))) * table[:, m : m + 1]
        factor = factor + table[:, 8 + m : 9 + m]
        result = factor if result is None else result * factor
    return result


def basis(coords, table):
    first, second, third = [lagrange(coords[d : d + 1], table) for d in range(3)]
    plane = jnp.concatenate([second[b : b + 1] * third for b in range(8)], axis=0)
    return jnp.concatenate([first[a : a + 1] * plane for a in range(8)], axis=0)


def kernel(
    z, axes, field_hbm, nbr_t_ref, cell_one_ref, ref_one_ref, cell_two_ref, ref_two_ref,
    vel_ref, rate_ref, cut_ref, own_hi_hbm, own_lo_hbm, sel_hbm, sel_t_hbm, table_ref,
    field_out_ref, vel_out_ref,
    field_ref, own_hi_ref, own_lo_ref, sel_ref, sel_t_ref,
    out_one, in_one, out_two, in_two, ret_out, ret_in, carry_out, carry_in, face_out, face_in,
    w_hi, w_lo, src, force_ref, mid_ref,
    a2a_send, a2a_recv, ret_send, ret_recv, face_send, face_recv, carry_sems, load_sems,
):
    loads = [
        pltpu.make_async_copy(here, there, load_sems.at[index])
        for index, (here, there) in enumerate(
            [
                (field_hbm, field_ref),
                (sel_hbm, sel_ref),
                (own_hi_hbm, own_hi_ref),
                (own_lo_hbm, own_lo_ref),
                (sel_t_hbm, sel_t_ref),
            ]
        )
    ]
    for load in loads:
        load.start()

    count_x, count_y, count_z = axes
    ix, iy, iz = lax.axis_index("gx"), lax.axis_index("gy"), lax.axis_index("gz")
    me = iy * count_z + iz
    elements, n_own = z.elements, z.owners
    base = ((ix * n_own + me) * elements).astype(jnp.int32)

    def member(index):
        return (ix, index // count_z, index % count_z)

    def peer(r):
        return lax.rem(me + r, n_own)

    barrier = pltpu.get_barrier_semaphore()

    def greet(r, _):
        pl.semaphore_signal(barrier, inc=1, device_id=member(peer(r)), device_id_type=MESH)
        return 0

    lax.fori_loop(1, n_own, greet, 0)
    up_x = (lax.rem(ix + 1, count_x), iy, iz)
    down_x = (lax.rem(ix + count_x - 1, count_x), iy, iz)
    for device in (up_x, down_x):
        pl.semaphore_signal(barrier, inc=1, device_id=device, device_id_type=MESH)

    def outgoing(stage):
        return (out_one, in_one) if stage == 0 else (out_two.at[stage - 1], in_two.at[stage - 1])

    def part_copy(stage, r):
        to = peer(r)
        source, target = outgoing(stage)
        return pltpu.make_async_remote_copy(
            src_ref=source.at[pl.ds(to * z.bpo, z.bpo)],
            dst_ref=target.at[pl.ds(me * z.bpo, z.bpo)],
            send_sem=a2a_send.at[stage, r],
            recv_sem=a2a_recv.at[stage, r],
            device_id=member(to),
            device_id_type=MESH,
        )

    def ret_copy(stage, r):
        to = peer(r)
        return pltpu.make_async_remote_copy(
            src_ref=ret_out.at[stage, to],
            dst_ref=ret_in.at[stage, me],
            send_sem=ret_send.at[stage, r],
            recv_sem=ret_recv.at[stage, r],
            device_id=member(to),
            device_id_type=MESH,
        )

    def start_all(make, stage):
        def body(r, _):
            make(stage, r).start()
            return 0

        lax.fori_loop(1, n_own, body, 0)

    def wait_all(make, stage):
        def body(r, _):
            make(stage, r).wait()
            return 0

        lax.fori_loop(1, n_own, body, 0)

    def send_parts(stage, packed):
        source, target = outgoing(stage)
        source[...] = packed
        own = pl.ds(me * z.bpo, z.bpo)
        target[own] = source[own]
        start_all(part_copy, stage)

    def take(stage, r):
        if z.opc == 1:
            part_copy(stage, r).wait()

    def give(stage, r):
        if z.opc == 1:
            ret_copy(stage, n_own - r).start()

    def take_all(stage):
        if z.opc > 1:
            wait_all(part_copy, stage)

    def give_all(stage):
        ret_in[stage, me] = ret_out[stage, me]
        if z.opc > 1:
            start_all(ret_copy, stage)

    def turn(r):
        return lax.rem(me + n_own - r, n_own) if z.opc == 1 else r

    face_devices = [
        down_x,
        up_x,
        (ix, lax.rem(iy + count_y - 1, count_y), iz),
        (ix, lax.rem(iy + 1, count_y), iz),
        (ix, iy, lax.rem(iz + count_z - 1, count_z)),
        (ix, iy, lax.rem(iz + 1, count_z)),
    ]

    def face_copy(stage, side):
        return pltpu.make_async_remote_copy(
            src_ref=face_out.at[stage, side],
            dst_ref=face_in.at[stage, side ^ 1],
            send_sem=face_send.at[stage, side],
            recv_sem=face_recv.at[stage, side ^ 1],
            device_id=face_devices[side],
            device_id_type=MESH,
        )

    def face_wait(stage):
        for side in range(6):
            face_copy(stage, side).wait_send()
        for side in range(6):
            pltpu.make_async_remote_copy(
                src_ref=face_out.at[stage, side ^ 1],
                dst_ref=face_in.at[stage, side],
                send_sem=face_send.at[stage, side ^ 1],
                recv_sem=face_recv.at[stage, side],
                device_id=face_devices[side],
                device_id_type=MESH,
            ).wait_recv()

    table = table_ref[...]

    rate = rate_ref[...]
    element, slot_one = place(z, cell_one_ref[...])
    packed = pack(
        z, jnp.concatenate([element + 1.0, ref_one_ref[...], vel_ref[...], rate], axis=0), slot_one
    )
    pl.semaphore_wait(barrier, n_own - 1 + 2)
    send_parts(0, packed)

    square = (elements, elements)
    rows = nbr_t_ref[...].astype(f32)
    columns = jnp.concatenate([rows, rows[:2]], axis=0).T
    base = base.astype(f32)
    compacts, partners = [], []
    for side in range(6):
        col = columns[:, side : side + 1]
        row = rows[side : side + 1, :]
        col_out = (col < base) | (col >= base + elements)
        row_out = (row < base) | (row >= base + elements)
        before = jnp.where(col_out & (iota(square, 0) < iota(square, 1)), 1.0, 0.0)
        before = jnp.sum(before, axis=0, keepdims=True)
        compact = onehot((fiota((z.edge, elements), 0) == before) & row_out).astype(b16)
        compacts.append(jnp.concatenate([compact, compact], axis=1))
        here = onehot(fiota(square, 1) == col - base).astype(b16)
        lower = jnp.where(row_out & (row >= 0) & (row < col), 1.0, 0.0)
        rank = jnp.sum(lower, axis=1, keepdims=True)
        far = onehot((fiota((elements, z.edge), 1) == rank) & col_out & (col >= 0)).astype(b16)
        partners.append(jnp.concatenate([here, here, far, far], axis=1))

    def split_state(state):
        return split2(state.reshape(4 * elements, 512))

    def send_faces(stage, hi, lo):
        both = mm(jnp.concatenate([hi, lo], axis=0), sel_ref[...])
        faces = both[: 4 * elements] + both[4 * elements :]
        wide = []
        for side in range(6):
            lanes = jnp.concatenate(
                [
                    faces[k * elements : (k + 1) * elements, side * 64 : (side + 1) * 64]
                    for k in range(4)
                ],
                axis=1,
            )
            pair = jnp.concatenate(split2(lanes), axis=0)
            wide.append(pair)
            face_out[stage, side] = mm(compacts[side], pair)
            face_copy(stage, side).start()
        return wide

    def own_part(state, hi, lo):
        both = mm(jnp.concatenate([hi, lo], axis=0), own_hi_ref[...])
        rows = 4 * elements
        return state + both[:rows] + both[rows:] + mm(hi, own_lo_ref[...])

    def partner_part(stage, wide):
        got = []
        for side in range(6):
            far = jnp.concatenate(split2(face_in[stage, side]), axis=0)
            got.append(mm(partners[side], jnp.concatenate([wide[side ^ 1], far], axis=0)))
        joined = jnp.concatenate(
            [
                jnp.concatenate([got[side][:, k * 64 : (k + 1) * 64] for side in range(6)], axis=1)
                for k in range(4)
            ],
            axis=0,
        )
        hi, lo = split2(joined)
        rows = 4 * elements
        both = mm(jnp.concatenate([hi, lo], axis=0), sel_t_ref[...])
        return penalty * (both[:rows] + both[rows:])

    def chunk_rows(ref, i):
        piece = ref[pl.ds(i * z.tpc, z.tpc)]
        return jnp.concatenate([piece[t] for t in range(z.tpc)], axis=1)

    def sample(places, hi, lo, i):
        w_up, w_down = split2(basis(places[1:4], table))
        w_hi[i] = w_up
        w_lo[i] = w_down
        rows = 3 * elements
        both = mm(jnp.concatenate([hi[:rows], lo[:rows]], axis=0), w_up)
        values = both[:rows] + both[rows:] + mm(hi[:rows], w_down)
        pick = fiota((elements, z.chunk), 0) == places[0:1] - 1.0
        return jnp.concatenate(
            [
                jnp.sum(
                    jnp.where(pick, values[k * elements : (k + 1) * elements], 0.0),
                    axis=0,
                    keepdims=True,
                )
                for k in range(3)
            ],
            axis=0,
        )

    def drag(stage, fluid, place_row, dynamic, i):
        speeds, rates = dynamic[:3], dynamic[3:4]
        offset = fluid - speeds
        accel = rates * offset
        heat = rates * jnp.sum(offset * offset, axis=0, keepdims=True)
        fresh = speeds + step_time * accel
        src[i] = jnp.concatenate(
            [couplings[0] * accel, couplings[3] * heat, place_row, fresh], axis=0
        )
        for j in range(z.opc):
            rows = []
            for v in range(3):
                for b in range(z.bpo):
                    at = j * z.cap + b * z.lw
                    rows.append(fresh[v : v + 1, at : at + z.lw])
            if z.rpb > 3 * z.bpo:
                rows.append(jnp.zeros((z.rpb - 3 * z.bpo, z.lw), f32))
            ret_out[stage, i * z.opc + j] = jnp.concatenate(rows, axis=0)

    def spread(i):
        data = src[i]
        pick = fiota((elements, z.chunk), 0) == data[4:5] - 1.0
        loads = jnp.concatenate([jnp.where(pick, data[k : k + 1], 0.0) for k in range(4)], axis=0)
        hi, lo = split2(loads)
        both = nt(w_hi[i], jnp.concatenate([hi, lo], axis=0))
        rows = 4 * elements
        return both[:, :rows] + both[:, rows:] + nt(w_lo[i], hi)

    for load in loads[:2]:
        load.wait()
    state = field_ref[...].reshape(4 * elements, 512)
    hi, lo = split2(state)
    wide = send_faces(0, hi, lo)

    element, slot_two = place(z, cell_two_ref[...])
    send_parts(
        1, pack(z, jnp.concatenate([element + 1.0, ref_two_ref[...]], axis=0), slot_two)
    )
    for load in loads[2:]:
        load.wait()
    mid_ref[...] = own_part(state, hi, lo)

    def first(i):
        data = chunk_rows(in_one, i)
        drag(0, sample(data[:4], hi, lo, i), data[0:1], data[4:], i)

    take_all(0)
    first(turn(0))
    force_ref[...] = jnp.zeros_like(force_ref)

    def first_step(r, _):
        take(0, r)
        force_ref[...] += spread(turn(r - 1))
        first(turn(r))
        give(0, r)
        return 0

    lax.fori_loop(1, z.chunks, first_step, 0)
    give_all(0)
    force = force_ref[...] + spread(turn(z.chunks - 1))
    mid_ref[...] += force.T
    face_wait(0)
    state = mid_ref[...] + partner_part(0, wide)
    hi, lo = split2(state)
    wide = send_faces(1, hi, lo)
    mid_ref[...] = own_part(state, hi, lo)
    wait_all(ret_copy, 0)
    carry_out[...] = jnp.concatenate([unpack(z, ret_in[0], slot_one), rate], axis=0)
    carry = pltpu.make_async_remote_copy(
        src_ref=carry_out,
        dst_ref=carry_in,
        send_sem=carry_sems.at[0],
        recv_sem=carry_sems.at[1],
        device_id=member(lax.rem(me + n_own - 1, n_own)),
        device_id_type=MESH,
    )
    carry.start()
    wait_all(part_copy, 1)

    def second(i):
        places = chunk_rows(in_two.at[0], i)
        src[i, 0:3] = sample(places, hi, lo, i)

    half = z.chunks // 2
    for i in range(half):
        second(i)
    carry.wait()
    moved = shift(z, jnp.concatenate([carry_out[...], carry_in[...]], axis=1), cut_ref[0])
    send_parts(2, pack(z, moved, slot_two))
    for i in range(half, z.chunks):
        second(i)
    force_ref[...] = jnp.zeros_like(force_ref)
    take_all(2)

    def finish(i):
        places = chunk_rows(in_two.at[0], i)
        drag(1, src[i, 0:3], places[0:1], chunk_rows(in_two.at[1], i), i)

    finish(turn(0))

    def second_step(r, _):
        take(2, r)
        finish(turn(r))
        give(1, r)
        force_ref[...] += spread(turn(r - 1))
        return 0

    lax.fori_loop(1, z.chunks, second_step, 0)
    give_all(1)
    force = force_ref[...] + spread(turn(z.chunks - 1))
    mid_ref[...] += force.T
    face_wait(1)
    final = mid_ref[...] + partner_part(1, wide)
    field_out_ref[...] = final.reshape(4, elements, 512)
    wait_all(ret_copy, 1)
    vel_out_ref[...] = unpack(z, ret_in[1], slot_two)


def local(axes, field, neighbours, cell_one, ref_one, cell_two, ref_two, velocity, rate, cut):
    elements, particles = field.shape[1], cell_one.shape[0]
    owners = axes[1] * axes[2]
    z = Sizes(owners, elements, particles)
    selection = face_table()
    own = viscosity * laplace_table() - penalty * np.diag(selection.sum(axis=1))
    own_hi = own.astype(np.float32).astype(b16)
    own_lo = (own - own_hi.astype(np.float64)).astype(np.float32).astype(b16)
    table = np.concatenate([gap_table(), np.eye(8)], axis=1).astype(np.float32)
    vmem = pl.BlockSpec(memory_space=pltpu.VMEM)
    args = [
        field,
        neighbours.T,
        cell_one[None],
        ref_one,
        cell_two[None],
        ref_two,
        velocity,
        rate[None],
        cut,
        jnp.asarray(own_hi),
        jnp.asarray(own_lo),
        jnp.asarray(selection, b16),
        jnp.asarray(selection.T, b16),
        jnp.asarray(table),
    ]
    specs = [vmem] * len(args)
    specs[8] = pl.BlockSpec(memory_space=pltpu.SMEM)
    for index in (0, 9, 10, 11, 12):
        specs[index] = pl.BlockSpec(memory_space=pl.ANY)
    dma = pltpu.SemaphoreType.DMA
    return pl.pallas_call(
        functools.partial(kernel, z, axes),
        out_shape=(
            jax.ShapeDtypeStruct(field.shape, f32),
            jax.ShapeDtypeStruct(velocity.shape, f32),
        ),
        in_specs=specs,
        out_specs=(vmem, vmem),
        scratch_shapes=[
            pltpu.VMEM(field.shape, f32),
            pltpu.VMEM((512, 512), b16),
            pltpu.VMEM((512, 512), b16),
            pltpu.VMEM((512, 384), b16),
            pltpu.VMEM((384, 512), b16),
            pltpu.VMEM((z.tiles, 8, z.lw), f32),
            pltpu.VMEM((z.tiles, 8, z.lw), f32),
            pltpu.VMEM((2, z.tiles, 4, z.lw), f32),
            pltpu.VMEM((2, z.tiles, 4, z.lw), f32),
            pltpu.VMEM((2, owners, z.rpb, z.lw), f32),
            pltpu.VMEM((2, owners, z.rpb, z.lw), f32),
            pltpu.VMEM((4, particles), f32),
            pltpu.VMEM((4, particles), f32),
            pltpu.VMEM((2, 6, z.edge, 256), f32),
            pltpu.VMEM((2, 6, z.edge, 256), f32),
            pltpu.VMEM((z.chunks, 512, z.chunk), b16),
            pltpu.VMEM((z.chunks, 512, z.chunk), b16),
            pltpu.VMEM((z.chunks, 8, z.chunk), f32),
            pltpu.VMEM((512, 4 * elements), f32),
            pltpu.VMEM((4 * elements, 512), f32),
            dma((3, owners)),
            dma((3, owners)),
            dma((2, owners)),
            dma((2, owners)),
            dma((2, 6)),
            dma((2, 6)),
            dma((2,)),
            dma((5,)),
        ],
        compiler_params=pltpu.CompilerParams(
            collective_id=0, has_side_effects=True, vmem_limit_bytes=56 * 1024 * 1024
        ),
    )(*args)


def solution(mesh):
    axes = (mesh.shape["gx"], mesh.shape["gy"], mesh.shape["gz"])
    in_specs = (
        P(None, ("gx", "gy", "gz"), None),
        P(("gx", "gy", "gz"), None),
        P(("gx", "gy", "gz")),
        P(None, ("gx", "gy", "gz")),
        P(("gx", "gy", "gz")),
        P(None, ("gx", "gy", "gz")),
        P(None, ("gx", "gy", "gz")),
        P(("gx", "gy", "gz")),
        P(),
    )
    out_specs = (P(None, ("gx", "gy", "gz"), None), P(None, ("gx", "gy", "gz")))
    return jax.shard_map(
        functools.partial(local, axes), mesh=mesh, in_specs=in_specs, out_specs=out_specs,
        check_vma=False,
    )
```

```python
import functools
import jax
import jax.numpy as jnp
import numpy as np
from jax import lax
from jax.experimental import pallas as pl
from jax.experimental.pallas import tpu as pltpu
from jax.sharding import PartitionSpec as P

EDGE = 4
node_points = -np.cos(np.pi * np.arange(8) / 7.0)
step_time = 0.1
viscosity = 0.002
penalty = 0.25
couplings = (-0.5, -0.5, -0.5, 0.5)
f32 = jnp.float32
b16 = jnp.bfloat16
MESH = pl.DeviceIdType.MESH


def gap_table():
    differences = node_points[:, None] - node_points[None, :] + np.eye(8)
    inverse = 1.0 / differences
    return inverse * (1.0 - np.eye(8))


def laplace_table():
    differences = node_points[:, None] - node_points[None, :] + np.eye(8)
    weights = 1.0 / np.prod(differences, axis=1)
    derivative = weights[None, :] / weights[:, None] / differences
    derivative = derivative * (1.0 - np.eye(8))
    derivative = derivative - np.eye(8) * derivative.sum(axis=1)[:, None]
    second = derivative @ derivative
    identity = np.eye(8)
    operator = np.kron(np.kron(second, identity), identity)
    operator = operator + np.kron(np.kron(identity, second), identity)
    operator = operator + np.kron(np.kron(identity, identity), second)
    return operator.T


def face_table():
    selection = np.zeros((512, 384))
    for side in range(6):
        edge = 0 if side % 2 == 0 else 7
        for row in range(8):
            for col in range(8):
                if side < 2:
                    node = (edge * 8 + row) * 8 + col
                elif side < 4:
                    node = (row * 8 + edge) * 8 + col
                else:
                    node = (row * 8 + col) * 8 + edge
                selection[node, side * 64 + row * 8 + col] = 1.0
    return selection


def mm(a, b):
    return lax.dot_general(a, b, (((1,), (0,)), ((), ())), preferred_element_type=f32)


def nt(a, b):
    return lax.dot_general(a, b, (((1,), (1,)), ((), ())), preferred_element_type=f32)


def split2(x):
    hi = x.astype(b16)
    return hi, (x - hi.astype(f32)).astype(b16)


def split3(x):
    hi = x.astype(b16)
    rest = x - hi.astype(f32)
    mid = rest.astype(b16)
    return hi, mid, (rest - mid.astype(f32)).astype(b16)


def iota(shape, dim):
    return lax.broadcasted_iota(jnp.int32, shape, dim)


def fiota(shape, dim):
    return iota(shape, dim).astype(f32)


def quotient(x, n):
    return jnp.floor((x + 0.5) * (1.0 / n))


def onehot(mask):
    return jnp.where(mask, 1.0, 0.0).astype(f32)


def widen(joined, sel_t):
    rows = joined.shape[0]
    both = mm(jnp.concatenate(split2(joined), axis=0), sel_t)
    return penalty * (both[:rows] + both[rows:])


def ending(mid_ref, joined_ref, vel_ref, sel_t_ref, field_out_ref, vel_out_ref):
    final = mid_ref[...] + widen(joined_ref[...], sel_t_ref[...])
    field_out_ref[...] = final.reshape(field_out_ref.shape)
    vel_out_ref[...] = vel_ref[...]


class Sizes:
    def __init__(self, owners, elements, particles):
        self.owners, self.elements, self.particles = owners, elements, particles
        self.cap = 2 * particles // owners
        self.lw = min(128, self.cap)
        self.bpo = self.cap // self.lw
        self.tiles = owners * self.bpo
        self.rpb = -(-3 * self.bpo // 8) * 8
        self.opc = max(1, 512 // self.cap)
        self.chunk = self.opc * self.cap
        self.tpc = self.opc * self.bpo
        self.chunks = owners // self.opc
        self.edge = EDGE * EDGE


def place(z, cell):
    number = cell.astype(f32)
    device = quotient(number, z.elements)
    element = number - device * z.elements
    owner = device - quotient(device, z.owners) * z.owners
    marks = onehot(fiota((z.owners, z.particles), 0) == owner)
    parts = z.particles // 128
    rows = parts * z.owners
    stacked = jnp.concatenate([marks[:, c * 128 : (c + 1) * 128] for c in range(parts)], axis=0)
    upper = onehot(iota((128, 128), 0) <= iota((128, 128), 1)).astype(b16)
    inside = mm(stacked.astype(b16), upper)
    totals = jnp.broadcast_to(inside[:, 127:128], (rows, 128)).astype(b16)
    row, col = fiota((rows, rows), 0), fiota((rows, rows), 1)
    row_part, col_part = quotient(row, z.owners), quotient(col, z.owners)
    same = (row - row_part * z.owners) == (col - col_part * z.owners)
    earlier = onehot(same & (col_part < row_part)).astype(b16)
    owner_of = fiota((rows, 128), 0)
    owner_of = owner_of - quotient(owner_of, z.owners) * z.owners
    value = stacked * (inside - 1.0 + mm(earlier, totals) + owner_of * z.cap)
    slot = jnp.concatenate(
        [
            jnp.sum(value[c * z.owners : (c + 1) * z.owners], axis=0, keepdims=True)
            for c in range(parts)
        ],
        axis=1,
    )
    return element, slot


def slot_parts(z, slot):
    high = quotient(slot, z.lw)
    low = slot - high * z.lw
    return high, onehot(fiota((z.lw, z.particles), 0) == low).astype(b16)


def pack(z, payload, slot):
    fields = payload.shape[0]
    high, low = slot_parts(z, slot)
    two = jnp.concatenate([part.astype(f32) for part in split2(payload)], axis=0)
    spread = jnp.concatenate(
        [jnp.where(high == float(i), two, 0.0) for i in range(z.tiles)], axis=0
    ).astype(b16)
    moved = nt(spread, low).reshape(z.tiles, 2 * fields, z.lw)
    return moved[:, :fields] + moved[:, fields:]


def unpack(z, block, slot):
    high, low = slot_parts(z, slot)
    rows = z.owners * z.rpb
    flat = block.reshape(rows, z.lw)
    got = mm(jnp.concatenate(split2(flat), axis=0), low)
    got = got[:rows] + got[rows:]
    row = fiota((z.rpb, z.particles), 0)
    key = high - (row - quotient(row, z.bpo) * z.bpo)
    total = jnp.zeros((z.rpb, z.particles), f32)
    for o in range(z.owners):
        total = total + jnp.where(
            key == float(o * z.bpo), got[o * z.rpb : (o + 1) * z.rpb], 0.0
        )
    return jnp.concatenate(
        [
            jnp.sum(total[v * z.bpo : (v + 1) * z.bpo], axis=0, keepdims=True)
            for v in range(3)
        ],
        axis=0,
    )


def shift(z, pair, cut):
    bit = 1 << (z.particles - 1).bit_length() - 1
    while bit >= 1:
        flag = jnp.full(pair.shape, (cut // bit) % 2, jnp.int32) == 1
        if bit >= 128:
            width = z.particles + bit
            pair = jnp.where(flag[:, :width], pair[:, bit : bit + width], pair[:, :width])
        else:
            pair = jnp.where(flag, pltpu.roll(pair, pair.shape[1] - bit, 1), pair)
        bit //= 2
    return pair[:, : z.particles]


def lagrange(x, table):
    result = None
    for m in range(8):
        factor = (x - float(np.float32(node_points[m]))) * table[:, m : m + 1]
        factor = factor + table[:, 8 + m : 9 + m]
        result = factor if result is None else result * factor
    return result


def basis(coords, table):
    first, second, third = [lagrange(coords[d : d + 1], table) for d in range(3)]
    plane = jnp.concatenate([second[b : b + 1] * third for b in range(8)], axis=0)
    return jnp.concatenate([first[a : a + 1] * plane for a in range(8)], axis=0)


def kernel(
    z, axes, field_hbm, nbr_t_ref, cell_one_ref, ref_one_ref, cell_two_ref, ref_two_ref,
    vel_ref, rate_ref, cut_ref, own_hi_hbm, own_lo_hbm, sel_hbm, sel_t_hbm, table_ref,
    mid_ref, joined_ref, vel_out_ref,
    field_ref, own_hi_ref, own_lo_ref, sel_ref, sel_t_ref,
    out_one, in_one, out_two, in_two, ret_out, ret_in, carry_out, carry_in, face_out, face_in,
    w_hi, w_lo, src, flow, force_ref,
    a2a_send, a2a_recv, ret_send, ret_recv, face_send, face_recv, carry_sems, load_sems,
):
    loads = [
        pltpu.make_async_copy(here, there, load_sems.at[index])
        for index, (here, there) in enumerate(
            [
                (field_hbm, field_ref),
                (sel_hbm, sel_ref),
                (own_hi_hbm, own_hi_ref),
                (own_lo_hbm, own_lo_ref),
                (sel_t_hbm, sel_t_ref),
            ]
        )
    ]
    for load in loads:
        load.start()

    count_x, count_y, count_z = axes
    ix, iy, iz = lax.axis_index("gx"), lax.axis_index("gy"), lax.axis_index("gz")
    me = iy * count_z + iz
    elements, n_own = z.elements, z.owners
    base = ((ix * n_own + me) * elements).astype(jnp.int32)

    def member(index):
        return (ix, index // count_z, index % count_z)

    def peer(r):
        return lax.rem(me + r, n_own)

    barrier = pltpu.get_barrier_semaphore()

    def greet(r, _):
        pl.semaphore_signal(barrier, inc=1, device_id=member(peer(r)), device_id_type=MESH)
        return 0

    lax.fori_loop(1, n_own, greet, 0)
    up_x = (lax.rem(ix + 1, count_x), iy, iz)
    down_x = (lax.rem(ix + count_x - 1, count_x), iy, iz)
    for device in (up_x, down_x):
        pl.semaphore_signal(barrier, inc=1, device_id=device, device_id_type=MESH)

    def outgoing(stage):
        return (out_one, in_one) if stage == 0 else (out_two.at[stage - 1], in_two.at[stage - 1])

    def part_copy(stage, r):
        to = peer(r)
        source, target = outgoing(stage)
        return pltpu.make_async_remote_copy(
            src_ref=source.at[pl.ds(to * z.bpo, z.bpo)],
            dst_ref=target.at[pl.ds(me * z.bpo, z.bpo)],
            send_sem=a2a_send.at[stage, r],
            recv_sem=a2a_recv.at[stage, r],
            device_id=member(to),
            device_id_type=MESH,
        )

    def ret_copy(stage, r):
        to = peer(r)
        return pltpu.make_async_remote_copy(
            src_ref=ret_out.at[stage, to],
            dst_ref=ret_in.at[stage, me],
            send_sem=ret_send.at[stage, r],
            recv_sem=ret_recv.at[stage, r],
            device_id=member(to),
            device_id_type=MESH,
        )

    def start_all(make, stage):
        def body(r, _):
            make(stage, r).start()
            return 0

        lax.fori_loop(1, n_own, body, 0)

    def wait_all(make, stage):
        def body(r, _):
            make(stage, r).wait()
            return 0

        lax.fori_loop(1, n_own, body, 0)

    def send_parts(stage, packed):
        source, target = outgoing(stage)
        source[...] = packed
        own = pl.ds(me * z.bpo, z.bpo)
        target[own] = source[own]
        start_all(part_copy, stage)

    def take(stage, r):
        if z.opc == 1:
            part_copy(stage, r).wait()

    def give(stage, r):
        if z.opc == 1:
            ret_copy(stage, n_own - r).start()

    def take_all(stage):
        if z.opc > 1:
            wait_all(part_copy, stage)

    def give_all(stage):
        ret_in[stage, me] = ret_out[stage, me]
        if z.opc > 1:
            start_all(ret_copy, stage)

    def turn(r):
        return lax.rem(me + n_own - r, n_own) if z.opc == 1 else r

    face_devices = [
        down_x,
        up_x,
        (ix, lax.rem(iy + count_y - 1, count_y), iz),
        (ix, lax.rem(iy + 1, count_y), iz),
        (ix, iy, lax.rem(iz + count_z - 1, count_z)),
        (ix, iy, lax.rem(iz + 1, count_z)),
    ]

    def face_copy(stage, side):
        return pltpu.make_async_remote_copy(
            src_ref=face_out.at[stage, side],
            dst_ref=face_in.at[stage, side ^ 1],
            send_sem=face_send.at[stage, side],
            recv_sem=face_recv.at[stage, side ^ 1],
            device_id=face_devices[side],
            device_id_type=MESH,
        )

    def face_wait(stage):
        for side in range(6):
            face_copy(stage, side).wait_send()
        for side in range(6):
            pltpu.make_async_remote_copy(
                src_ref=face_out.at[stage, side ^ 1],
                dst_ref=face_in.at[stage, side],
                send_sem=face_send.at[stage, side ^ 1],
                recv_sem=face_recv.at[stage, side],
                device_id=face_devices[side],
                device_id_type=MESH,
            ).wait_recv()

    table = table_ref[...]

    rate = rate_ref[...]
    element, slot_one = place(z, cell_one_ref[...])
    packed = pack(
        z, jnp.concatenate([element + 1.0, ref_one_ref[...], vel_ref[...], rate], axis=0), slot_one
    )
    pl.semaphore_wait(barrier, n_own - 1 + 2)
    send_parts(0, packed)

    square = (elements, elements)
    rows = nbr_t_ref[...].astype(f32)
    columns = jnp.concatenate([rows, rows[:2]], axis=0).T
    base = base.astype(f32)
    compacts, partners = [], []
    for side in range(6):
        col = columns[:, side : side + 1]
        row = rows[side : side + 1, :]
        col_out = (col < base) | (col >= base + elements)
        row_out = (row < base) | (row >= base + elements)
        before = jnp.where(col_out & (iota(square, 0) < iota(square, 1)), 1.0, 0.0)
        before = jnp.sum(before, axis=0, keepdims=True)
        compact = onehot((fiota((z.edge, elements), 0) == before) & row_out).astype(b16)
        compacts.append(jnp.concatenate([compact, compact], axis=1))
        here = onehot(fiota(square, 1) == col - base).astype(b16)
        lower = jnp.where(row_out & (row >= 0) & (row < col), 1.0, 0.0)
        rank = jnp.sum(lower, axis=1, keepdims=True)
        far = onehot((fiota((elements, z.edge), 1) == rank) & col_out & (col >= 0)).astype(b16)
        partners.append(jnp.concatenate([here, here, far, far], axis=1))

    def split_state(state):
        return split2(state.reshape(4 * elements, 512))

    def send_faces(stage, hi, lo):
        both = mm(jnp.concatenate([hi, lo], axis=0), sel_ref[...])
        faces = both[: 4 * elements] + both[4 * elements :]
        wide = []
        for side in range(6):
            lanes = jnp.concatenate(
                [
                    faces[k * elements : (k + 1) * elements, side * 64 : (side + 1) * 64]
                    for k in range(4)
                ],
                axis=1,
            )
            pair = jnp.concatenate(split2(lanes), axis=0)
            wide.append(pair)
            face_out[stage, side] = mm(compacts[side], pair)
            face_copy(stage, side).start()
        return wide

    def own_part(state, hi, lo):
        both = mm(jnp.concatenate([hi, lo], axis=0), own_hi_ref[...])
        rows = 4 * elements
        return state + both[:rows] + both[rows:] + mm(hi, own_lo_ref[...])

    def partner_faces(stage, wide):
        got = []
        for side in range(6):
            far = jnp.concatenate(split2(face_in[stage, side]), axis=0)
            got.append(mm(partners[side], jnp.concatenate([wide[side ^ 1], far], axis=0)))
        return jnp.concatenate(
            [
                jnp.concatenate([got[side][:, k * 64 : (k + 1) * 64] for side in range(6)], axis=1)
                for k in range(4)
            ],
            axis=0,
        )

    def chunk_rows(ref, i):
        piece = ref[pl.ds(i * z.tpc, z.tpc)]
        return jnp.concatenate([piece[t] for t in range(z.tpc)], axis=1)

    def build(places, slot):
        w_up, w_down = split2(basis(places[1:4], table))
        w_hi[slot] = w_up
        w_lo[slot] = w_down
        return w_up, w_down

    def sample(places, hi, lo, w_up, w_down):
        rows = 3 * elements
        both = mm(jnp.concatenate([hi[:rows], lo[:rows]], axis=0), w_up)
        values = both[:rows] + both[rows:] + mm(hi[:rows], w_down)
        pick = fiota((elements, z.chunk), 0) == places[0:1] - 1.0
        return jnp.concatenate(
            [
                jnp.sum(
                    jnp.where(pick, values[k * elements : (k + 1) * elements], 0.0),
                    axis=0,
                    keepdims=True,
                )
                for k in range(3)
            ],
            axis=0,
        )

    def drag(stage, fluid, place_row, dynamic, i, at_src):
        speeds, rates = dynamic[:3], dynamic[3:4]
        offset = fluid - speeds
        accel = rates * offset
        heat = rates * jnp.sum(offset * offset, axis=0, keepdims=True)
        fresh = speeds + step_time * accel
        src[at_src] = jnp.concatenate(
            [couplings[0] * accel, couplings[3] * heat, place_row, fresh], axis=0
        )
        for j in range(z.opc):
            rows = []
            for v in range(3):
                for b in range(z.bpo):
                    at = j * z.cap + b * z.lw
                    rows.append(fresh[v : v + 1, at : at + z.lw])
            if z.rpb > 3 * z.bpo:
                rows.append(jnp.zeros((z.rpb - 3 * z.bpo, z.lw), f32))
            ret_out[stage, i * z.opc + j] = jnp.concatenate(rows, axis=0)

    def spread(at_src, at_w):
        data = src[at_src]
        pick = fiota((elements, z.chunk), 0) == data[4:5] - 1.0
        loads = jnp.concatenate([jnp.where(pick, data[k : k + 1], 0.0) for k in range(4)], axis=0)
        hi, lo = split2(loads)
        both = nt(w_hi[at_w], jnp.concatenate([hi, lo], axis=0))
        rows = 4 * elements
        force = both[:, :rows] + both[:, rows:] + nt(w_lo[at_w], hi)
        if at_src == 0:
            force_ref[...] = force
        else:
            force_ref[...] += force

    for load in loads[:2]:
        load.wait()
    state = field_ref[...].reshape(4 * elements, 512)
    hi, lo = split2(state)
    wide = send_faces(0, hi, lo)

    element, slot_two = place(z, cell_two_ref[...])
    send_parts(
        1, pack(z, jnp.concatenate([element + 1.0, ref_two_ref[...]], axis=0), slot_two)
    )
    for load in loads[2:]:
        load.wait()
    mid_ref[...] = own_part(state, hi, lo)

    def first(r):
        data = chunk_rows(in_one, turn(r))
        fluid = sample(data[:4], hi, lo, w_hi[r], w_lo[r])
        drag(0, fluid, data[0:1], data[4:], turn(r), r)

    take_all(0)
    for r in range(z.chunks + 2):
        if 0 < r < z.chunks:
            take(0, r)
        if r >= 2:
            spread(r - 2, r - 2)
        if 1 <= r <= z.chunks:
            first(r - 1)
        if r < z.chunks:
            build(chunk_rows(in_one, turn(r))[:4], r)
        if 1 < r <= z.chunks:
            give(0, r - 1)
    give_all(0)
    mid_ref[...] += force_ref[...].T
    face_wait(0)
    state = mid_ref[...] + widen(partner_faces(0, wide), sel_t_ref[...])
    hi, lo = split2(state)
    wide = send_faces(1, hi, lo)
    mid_ref[...] = own_part(state, hi, lo)
    wait_all(ret_copy, 0)
    carry_out[...] = jnp.concatenate([unpack(z, ret_in[0], slot_one), rate], axis=0)
    carry = pltpu.make_async_remote_copy(
        src_ref=carry_out,
        dst_ref=carry_in,
        send_sem=carry_sems.at[0],
        recv_sem=carry_sems.at[1],
        device_id=member(lax.rem(me + n_own - 1, n_own)),
        device_id_type=MESH,
    )
    carry.start()
    wait_all(part_copy, 1)

    def second(i):
        places = chunk_rows(in_two.at[0], i)
        flow[i, 0:3] = sample(places, hi, lo, *build(places, i))

    half = z.chunks // 2
    for i in range(half):
        second(i)
    carry.wait()
    moved = shift(z, jnp.concatenate([carry_out[...], carry_in[...]], axis=1), cut_ref[0])
    send_parts(2, pack(z, moved, slot_two))
    for i in range(half, z.chunks):
        second(i)
    take_all(2)

    def finish(r):
        i = turn(r)
        places = chunk_rows(in_two.at[0], i)
        drag(1, flow[i, 0:3], places[0:1], chunk_rows(in_two.at[1], i), i, r)

    for r in range(z.chunks + 1):
        if 0 < r < z.chunks:
            take(2, r)
        if r < z.chunks:
            finish(r)
        if r >= 1:
            spread(r - 1, turn(r - 1))
        if 0 < r < z.chunks:
            give(1, r)
    give_all(1)
    mid_ref[...] += force_ref[...].T
    face_wait(1)
    joined_ref[...] = partner_faces(1, wide)
    wait_all(ret_copy, 1)
    vel_out_ref[...] = unpack(z, ret_in[1], slot_two)


def local(axes, field, neighbours, cell_one, ref_one, cell_two, ref_two, velocity, rate, cut):
    elements, particles = field.shape[1], cell_one.shape[0]
    owners = axes[1] * axes[2]
    z = Sizes(owners, elements, particles)
    selection = face_table()
    own = viscosity * laplace_table() - penalty * np.diag(selection.sum(axis=1))
    own_hi = own.astype(np.float32).astype(b16)
    own_lo = (own - own_hi.astype(np.float64)).astype(np.float32).astype(b16)
    table = np.concatenate([gap_table(), np.eye(8)], axis=1).astype(np.float32)
    vmem = pl.BlockSpec(memory_space=pltpu.VMEM)
    args = [
        field,
        neighbours.T,
        cell_one[None],
        ref_one,
        cell_two[None],
        ref_two,
        velocity,
        rate[None],
        cut,
        jnp.asarray(own_hi),
        jnp.asarray(own_lo),
        jnp.asarray(selection, b16),
        jnp.asarray(selection.T, b16),
        jnp.asarray(table),
    ]
    specs = [vmem] * len(args)
    specs[8] = pl.BlockSpec(memory_space=pltpu.SMEM)
    for index in (0, 9, 10, 11, 12):
        specs[index] = pl.BlockSpec(memory_space=pl.ANY)
    dma = pltpu.SemaphoreType.DMA
    mid, joined, speeds = pl.pallas_call(
        functools.partial(kernel, z, axes),
        out_shape=(
            jax.ShapeDtypeStruct((4 * elements, 512), f32),
            jax.ShapeDtypeStruct((4 * elements, 384), f32),
            jax.ShapeDtypeStruct(velocity.shape, f32),
        ),
        in_specs=specs,
        out_specs=(vmem, vmem, vmem),
        scratch_shapes=[
            pltpu.VMEM(field.shape, f32),
            pltpu.VMEM((512, 512), b16),
            pltpu.VMEM((512, 512), b16),
            pltpu.VMEM((512, 384), b16),
            pltpu.VMEM((384, 512), b16),
            pltpu.VMEM((z.tiles, 8, z.lw), f32),
            pltpu.VMEM((z.tiles, 8, z.lw), f32),
            pltpu.VMEM((2, z.tiles, 4, z.lw), f32),
            pltpu.VMEM((2, z.tiles, 4, z.lw), f32),
            pltpu.VMEM((2, owners, z.rpb, z.lw), f32),
            pltpu.VMEM((2, owners, z.rpb, z.lw), f32),
            pltpu.VMEM((4, particles), f32),
            pltpu.VMEM((4, particles), f32),
            pltpu.VMEM((2, 6, z.edge, 256), f32),
            pltpu.VMEM((2, 6, z.edge, 256), f32),
            pltpu.VMEM((z.chunks, 512, z.chunk), b16),
            pltpu.VMEM((z.chunks, 512, z.chunk), b16),
            pltpu.VMEM((z.chunks, 8, z.chunk), f32),
            pltpu.VMEM((z.chunks, 8, z.chunk), f32),
            pltpu.VMEM((512, 4 * elements), f32),
            dma((3, owners)),
            dma((3, owners)),
            dma((2, owners)),
            dma((2, owners)),
            dma((2, 6)),
            dma((2, 6)),
            dma((2,)),
            dma((5,)),
        ],
        compiler_params=pltpu.CompilerParams(
            collective_id=0, has_side_effects=True, vmem_limit_bytes=56 * 1024 * 1024
        ),
    )(*args)
    return pl.pallas_call(
        ending,
        out_shape=(
            jax.ShapeDtypeStruct(field.shape, f32),
            jax.ShapeDtypeStruct(velocity.shape, f32),
        ),
        in_specs=[vmem] * 4,
        out_specs=(vmem, vmem),
        compiler_params=pltpu.CompilerParams(vmem_limit_bytes=32 * 1024 * 1024),
    )(mid, joined, speeds, args[12])


def solution(mesh):
    axes = (mesh.shape["gx"], mesh.shape["gy"], mesh.shape["gz"])
    in_specs = (
        P(None, ("gx", "gy", "gz"), None),
        P(("gx", "gy", "gz"), None),
        P(("gx", "gy", "gz")),
        P(None, ("gx", "gy", "gz")),
        P(("gx", "gy", "gz")),
        P(None, ("gx", "gy", "gz")),
        P(None, ("gx", "gy", "gz")),
        P(("gx", "gy", "gz")),
        P(),
    )
    out_specs = (P(None, ("gx", "gy", "gz"), None), P(None, ("gx", "gy", "gz")))
    return jax.shard_map(
        functools.partial(local, axes), mesh=mesh, in_specs=in_specs, out_specs=out_specs,
        check_vma=False,
    )
```

```python
import functools
import jax
import jax.numpy as jnp
import numpy as np
from jax import lax
from jax.experimental import pallas as pl
from jax.experimental.pallas import tpu as pltpu
from jax.sharding import PartitionSpec as P

EDGE = 4
node_points = -np.cos(np.pi * np.arange(8) / 7.0)
step_time = 0.1
viscosity = 0.002
penalty = 0.25
couplings = (-0.5, -0.5, -0.5, 0.5)
f32 = jnp.float32
b16 = jnp.bfloat16
MESH = pl.DeviceIdType.MESH


def gap_table():
    differences = node_points[:, None] - node_points[None, :] + np.eye(8)
    inverse = 1.0 / differences
    return inverse * (1.0 - np.eye(8))


def laplace_table():
    differences = node_points[:, None] - node_points[None, :] + np.eye(8)
    weights = 1.0 / np.prod(differences, axis=1)
    derivative = weights[None, :] / weights[:, None] / differences
    derivative = derivative * (1.0 - np.eye(8))
    derivative = derivative - np.eye(8) * derivative.sum(axis=1)[:, None]
    second = derivative @ derivative
    identity = np.eye(8)
    operator = np.kron(np.kron(second, identity), identity)
    operator = operator + np.kron(np.kron(identity, second), identity)
    operator = operator + np.kron(np.kron(identity, identity), second)
    return operator.T


def face_table():
    selection = np.zeros((512, 384))
    for side in range(6):
        edge = 0 if side % 2 == 0 else 7
        for row in range(8):
            for col in range(8):
                if side < 2:
                    node = (edge * 8 + row) * 8 + col
                elif side < 4:
                    node = (row * 8 + edge) * 8 + col
                else:
                    node = (row * 8 + col) * 8 + edge
                selection[node, side * 64 + row * 8 + col] = 1.0
    return selection


def mm(a, b):
    return lax.dot_general(a, b, (((1,), (0,)), ((), ())), preferred_element_type=f32)


def nt(a, b):
    return lax.dot_general(a, b, (((1,), (1,)), ((), ())), preferred_element_type=f32)


def split2(x):
    hi = x.astype(b16)
    return hi, (x - hi.astype(f32)).astype(b16)


def split3(x):
    hi = x.astype(b16)
    rest = x - hi.astype(f32)
    mid = rest.astype(b16)
    return hi, mid, (rest - mid.astype(f32)).astype(b16)


def iota(shape, dim):
    return lax.broadcasted_iota(jnp.int32, shape, dim)


def fiota(shape, dim):
    return iota(shape, dim).astype(f32)


def quotient(x, n):
    return jnp.floor((x + 0.5) * (1.0 / n))


def onehot(mask):
    return jnp.where(mask, 1.0, 0.0).astype(f32)


def widen(joined, sel_t):
    rows = joined.shape[0]
    both = mm(jnp.concatenate(split2(joined), axis=0), sel_t)
    return penalty * (both[:rows] + both[rows:])


def ending(mid_ref, joined_ref, vel_ref, sel_t_ref, field_out_ref, vel_out_ref):
    final = mid_ref[...] + widen(joined_ref[...], sel_t_ref[...])
    field_out_ref[...] = final.reshape(field_out_ref.shape)
    vel_out_ref[...] = vel_ref[...]


class Sizes:
    def __init__(self, owners, elements, particles):
        self.owners, self.elements, self.particles = owners, elements, particles
        self.cap = 2 * particles // owners
        self.lw = min(128, self.cap)
        self.bpo = self.cap // self.lw
        self.tiles = owners * self.bpo
        self.rpb = -(-3 * self.bpo // 8) * 8
        self.opc = max(1, 512 // self.cap)
        self.chunk = self.opc * self.cap
        self.tpc = self.opc * self.bpo
        self.chunks = owners // self.opc
        self.edge = EDGE * EDGE


def place(z, cell):
    number = cell.astype(f32)
    device = quotient(number, z.elements)
    element = number - device * z.elements
    owner = device - quotient(device, z.owners) * z.owners
    marks = onehot(fiota((z.owners, z.particles), 0) == owner)
    parts = z.particles // 128
    rows = parts * z.owners
    stacked = jnp.concatenate([marks[:, c * 128 : (c + 1) * 128] for c in range(parts)], axis=0)
    upper = onehot(iota((128, 128), 0) <= iota((128, 128), 1)).astype(b16)
    inside = mm(stacked.astype(b16), upper)
    totals = jnp.broadcast_to(inside[:, 127:128], (rows, 128)).astype(b16)
    row, col = fiota((rows, rows), 0), fiota((rows, rows), 1)
    row_part, col_part = quotient(row, z.owners), quotient(col, z.owners)
    same = (row - row_part * z.owners) == (col - col_part * z.owners)
    earlier = onehot(same & (col_part < row_part)).astype(b16)
    owner_of = fiota((rows, 128), 0)
    owner_of = owner_of - quotient(owner_of, z.owners) * z.owners
    value = stacked * (inside - 1.0 + mm(earlier, totals) + owner_of * z.cap)
    slot = jnp.concatenate(
        [
            jnp.sum(value[c * z.owners : (c + 1) * z.owners], axis=0, keepdims=True)
            for c in range(parts)
        ],
        axis=1,
    )
    return element, slot


def slot_parts(z, slot):
    high = quotient(slot, z.lw)
    low = slot - high * z.lw
    return high, onehot(fiota((z.lw, slot.shape[1]), 0) == low).astype(b16)


def over_lanes(z, body, start):
    step = min(512, z.particles)
    return lax.fori_loop(
        0, z.particles // step, lambda c, acc: body(pl.ds(c * step, step), acc), start
    )


def pack(z, payload, rows_ref, slot):
    fields = payload.shape[0]
    rows_ref[0:fields] = payload
    rows_ref[8:9] = slot

    def body(lanes, total):
        high, low = slot_parts(z, rows_ref[8:9, lanes])
        parts = split2(rows_ref[0:fields, lanes])
        two = jnp.concatenate([part.astype(f32) for part in parts], axis=0)
        spread = jnp.concatenate(
            [jnp.where(high == float(i), two, 0.0) for i in range(z.tiles)], axis=0
        )
        return total + nt(spread.astype(b16), low)

    moved = over_lanes(z, body, jnp.zeros((z.tiles * 2 * fields, z.lw), f32))
    moved = moved.reshape(z.tiles, 2 * fields, z.lw)
    return moved[:, :fields] + moved[:, fields:]


def unpack(z, block, rows_ref, slot, target_ref):
    rows = z.owners * z.rpb
    flat = jnp.concatenate(split2(block.reshape(rows, z.lw)), axis=0)
    rows_ref[8:9] = slot

    def body(lanes, _):
        high, low = slot_parts(z, rows_ref[8:9, lanes])
        got = mm(flat, low)
        got = got[:rows] + got[rows:]
        row = fiota((z.rpb, low.shape[1]), 0)
        key = high - (row - quotient(row, z.bpo) * z.bpo)
        total = jnp.zeros(key.shape, f32)
        for o in range(z.owners):
            total = total + jnp.where(
                key == float(o * z.bpo), got[o * z.rpb : (o + 1) * z.rpb], 0.0
            )
        target_ref[0:3, lanes] = jnp.concatenate(
            [
                jnp.sum(total[v * z.bpo : (v + 1) * z.bpo], axis=0, keepdims=True)
                for v in range(3)
            ],
            axis=0,
        )
        return 0

    over_lanes(z, body, 0)


def shift(z, pair, cut):
    bit = 1 << (z.particles - 1).bit_length() - 1
    while bit >= 1:
        flag = jnp.full(pair.shape, (cut // bit) % 2, jnp.int32) == 1
        if bit >= 128:
            width = z.particles + bit
            pair = jnp.where(flag[:, :width], pair[:, bit : bit + width], pair[:, :width])
        else:
            pair = jnp.where(flag, pltpu.roll(pair, pair.shape[1] - bit, 1), pair)
        bit //= 2
    return pair[:, : z.particles]


def lagrange(x, table):
    result = None
    for m in range(8):
        factor = (x - float(np.float32(node_points[m]))) * table[:, m : m + 1]
        factor = factor + table[:, 8 + m : 9 + m]
        result = factor if result is None else result * factor
    return result


def basis(coords, table):
    first, second, third = [lagrange(coords[d : d + 1], table) for d in range(3)]
    plane = jnp.concatenate([second[b : b + 1] * third for b in range(8)], axis=0)
    return jnp.concatenate([first[a : a + 1] * plane for a in range(8)], axis=0)


def kernel(
    z, axes, field_hbm, nbr_t_ref, cell_one_ref, ref_one_ref, cell_two_ref, ref_two_ref,
    vel_ref, rate_ref, cut_ref, own_hi_hbm, own_lo_hbm, sel_hbm, sel_t_hbm, table_ref,
    mid_ref, joined_ref, vel_out_ref,
    field_ref, own_hi_ref, own_lo_ref, sel_ref, sel_t_ref,
    out_one, in_one, out_two, in_two, ret_out, ret_in, carry_out, carry_in, face_out, face_in,
    w_hi, w_lo, src, flow, force_ref, low_ref,
    a2a_send, a2a_recv, ret_send, ret_recv, face_send, face_recv, carry_sems, load_sems,
):
    loads = [
        pltpu.make_async_copy(here, there, load_sems.at[index])
        for index, (here, there) in enumerate(
            [
                (field_hbm, field_ref),
                (sel_hbm, sel_ref),
                (own_hi_hbm, own_hi_ref),
                (own_lo_hbm, own_lo_ref),
                (sel_t_hbm, sel_t_ref),
            ]
        )
    ]
    for load in loads:
        load.start()

    count_x, count_y, count_z = axes
    ix, iy, iz = lax.axis_index("gx"), lax.axis_index("gy"), lax.axis_index("gz")
    me = iy * count_z + iz
    elements, n_own = z.elements, z.owners
    base = ((ix * n_own + me) * elements).astype(jnp.int32)

    def member(index):
        return (ix, index // count_z, index % count_z)

    def peer(r):
        return lax.rem(me + r, n_own)

    barrier = pltpu.get_barrier_semaphore()

    def greet(r, _):
        pl.semaphore_signal(barrier, inc=1, device_id=member(peer(r)), device_id_type=MESH)
        return 0

    lax.fori_loop(1, n_own, greet, 0)
    up_x = (lax.rem(ix + 1, count_x), iy, iz)
    down_x = (lax.rem(ix + count_x - 1, count_x), iy, iz)
    for device in (up_x, down_x):
        pl.semaphore_signal(barrier, inc=1, device_id=device, device_id_type=MESH)

    def outgoing(stage):
        return (out_one, in_one) if stage == 0 else (out_two.at[stage - 1], in_two.at[stage - 1])

    def part_copy(stage, r):
        to = peer(r)
        source, target = outgoing(stage)
        return pltpu.make_async_remote_copy(
            src_ref=source.at[pl.ds(to * z.bpo, z.bpo)],
            dst_ref=target.at[pl.ds(me * z.bpo, z.bpo)],
            send_sem=a2a_send.at[stage, r],
            recv_sem=a2a_recv.at[stage, r],
            device_id=member(to),
            device_id_type=MESH,
        )

    def ret_copy(stage, r):
        to = peer(r)
        return pltpu.make_async_remote_copy(
            src_ref=ret_out.at[stage, to],
            dst_ref=ret_in.at[stage, me],
            send_sem=ret_send.at[stage, r],
            recv_sem=ret_recv.at[stage, r],
            device_id=member(to),
            device_id_type=MESH,
        )

    def start_all(make, stage):
        def body(r, _):
            make(stage, r).start()
            return 0

        lax.fori_loop(1, n_own, body, 0)

    def wait_all(make, stage):
        def body(r, _):
            make(stage, r).wait()
            return 0

        lax.fori_loop(1, n_own, body, 0)

    def send_parts(stage, packed):
        source, target = outgoing(stage)
        source[...] = packed
        own = pl.ds(me * z.bpo, z.bpo)
        target[own] = source[own]
        start_all(part_copy, stage)

    def take(stage, r):
        if z.opc == 1:
            part_copy(stage, r).wait()

    def give(stage, r):
        if z.opc == 1:
            ret_copy(stage, n_own - r).start()

    def take_all(stage):
        if z.opc > 1:
            wait_all(part_copy, stage)

    def give_all(stage):
        ret_in[stage, me] = ret_out[stage, me]
        if z.opc > 1:
            start_all(ret_copy, stage)

    def turn(r):
        return lax.rem(me + n_own - r, n_own) if z.opc == 1 else r

    face_devices = [
        down_x,
        up_x,
        (ix, lax.rem(iy + count_y - 1, count_y), iz),
        (ix, lax.rem(iy + 1, count_y), iz),
        (ix, iy, lax.rem(iz + count_z - 1, count_z)),
        (ix, iy, lax.rem(iz + 1, count_z)),
    ]

    def face_copy(stage, side):
        return pltpu.make_async_remote_copy(
            src_ref=face_out.at[stage, side],
            dst_ref=face_in.at[stage, side ^ 1],
            send_sem=face_send.at[stage, side],
            recv_sem=face_recv.at[stage, side ^ 1],
            device_id=face_devices[side],
            device_id_type=MESH,
        )

    def face_wait(stage):
        for side in range(6):
            face_copy(stage, side).wait_send()
        for side in range(6):
            pltpu.make_async_remote_copy(
                src_ref=face_out.at[stage, side ^ 1],
                dst_ref=face_in.at[stage, side],
                send_sem=face_send.at[stage, side ^ 1],
                recv_sem=face_recv.at[stage, side],
                device_id=face_devices[side],
                device_id_type=MESH,
            ).wait_recv()

    table = table_ref[...]

    rate = rate_ref[...]
    element, slot_one = place(z, cell_one_ref[...])
    payload = jnp.concatenate([element + 1.0, ref_one_ref[...], vel_ref[...], rate], axis=0)
    packed = pack(z, payload, low_ref, slot_one)
    pl.semaphore_wait(barrier, n_own - 1 + 2)
    send_parts(0, packed)

    square = (elements, elements)
    rows = nbr_t_ref[...].astype(f32)
    columns = jnp.concatenate([rows, rows[:2]], axis=0).T
    base = base.astype(f32)
    compacts, partners = [], []
    for side in range(6):
        col = columns[:, side : side + 1]
        row = rows[side : side + 1, :]
        col_out = (col < base) | (col >= base + elements)
        row_out = (row < base) | (row >= base + elements)
        before = jnp.where(col_out & (iota(square, 0) < iota(square, 1)), 1.0, 0.0)
        before = jnp.sum(before, axis=0, keepdims=True)
        compact = onehot((fiota((z.edge, elements), 0) == before) & row_out).astype(b16)
        compacts.append(jnp.concatenate([compact, compact], axis=1))
        here = onehot(fiota(square, 1) == col - base).astype(b16)
        lower = jnp.where(row_out & (row >= 0) & (row < col), 1.0, 0.0)
        rank = jnp.sum(lower, axis=1, keepdims=True)
        far = onehot((fiota((elements, z.edge), 1) == rank) & col_out & (col >= 0)).astype(b16)
        partners.append(jnp.concatenate([here, here, far, far], axis=1))

    def split_state(state):
        return split2(state.reshape(4 * elements, 512))

    def send_faces(stage, hi, lo):
        both = mm(jnp.concatenate([hi, lo], axis=0), sel_ref[...])
        faces = both[: 4 * elements] + both[4 * elements :]
        wide = []
        for side in range(6):
            lanes = jnp.concatenate(
                [
                    faces[k * elements : (k + 1) * elements, side * 64 : (side + 1) * 64]
                    for k in range(4)
                ],
                axis=1,
            )
            pair = jnp.concatenate(split2(lanes), axis=0)
            wide.append(pair)
            face_out[stage, side] = mm(compacts[side], pair)
            face_copy(stage, side).start()
        return wide

    def own_part(state, hi, lo):
        both = mm(jnp.concatenate([hi, lo], axis=0), own_hi_ref[...])
        rows = 4 * elements
        return state + both[:rows] + both[rows:] + mm(hi, own_lo_ref[...])

    def partner_faces(stage, wide):
        got = []
        for side in range(6):
            far = jnp.concatenate(split2(face_in[stage, side]), axis=0)
            got.append(mm(partners[side], jnp.concatenate([wide[side ^ 1], far], axis=0)))
        return jnp.concatenate(
            [
                jnp.concatenate([got[side][:, k * 64 : (k + 1) * 64] for side in range(6)], axis=1)
                for k in range(4)
            ],
            axis=0,
        )

    def chunk_rows(ref, i):
        piece = ref[pl.ds(i * z.tpc, z.tpc)]
        return jnp.concatenate([piece[t] for t in range(z.tpc)], axis=1)

    def build(places, slot):
        w_up, w_down = split2(basis(places[1:4], table))
        w_hi[slot] = w_up
        w_lo[slot] = w_down
        return w_up, w_down

    def sample(places, hi, lo, w_up, w_down):
        rows = 3 * elements
        both = mm(jnp.concatenate([hi[:rows], lo[:rows]], axis=0), w_up)
        values = both[:rows] + both[rows:] + mm(hi[:rows], w_down)
        pick = fiota((elements, z.chunk), 0) == places[0:1] - 1.0
        return jnp.concatenate(
            [
                jnp.sum(
                    jnp.where(pick, values[k * elements : (k + 1) * elements], 0.0),
                    axis=0,
                    keepdims=True,
                )
                for k in range(3)
            ],
            axis=0,
        )

    def drag(stage, fluid, place_row, dynamic, i):
        speeds, rates = dynamic[:3], dynamic[3:4]
        offset = fluid - speeds
        accel = rates * offset
        heat = rates * jnp.sum(offset * offset, axis=0, keepdims=True)
        fresh = speeds + step_time * accel
        src[i] = jnp.concatenate(
            [couplings[0] * accel, couplings[3] * heat, place_row, fresh], axis=0
        )
        for j in range(z.opc):
            rows = []
            for v in range(3):
                for b in range(z.bpo):
                    at = j * z.cap + b * z.lw
                    rows.append(fresh[v : v + 1, at : at + z.lw])
            if z.rpb > 3 * z.bpo:
                rows.append(jnp.zeros((z.rpb - 3 * z.bpo, z.lw), f32))
            ret_out[stage, i * z.opc + j] = jnp.concatenate(rows, axis=0)

    def spread(i):
        data = src[i]
        pick = fiota((elements, z.chunk), 0) == data[4:5] - 1.0
        loads = jnp.concatenate([jnp.where(pick, data[k : k + 1], 0.0) for k in range(4)], axis=0)
        hi, lo = split2(loads)
        both = nt(w_hi[i], jnp.concatenate([hi, lo], axis=0))
        rows = 4 * elements
        force_ref[...] += both[:, :rows] + both[:, rows:] + nt(w_lo[i], hi)

    for load in loads[:2]:
        load.wait()
    state = field_ref[...].reshape(4 * elements, 512)
    hi, lo = split2(state)
    wide = send_faces(0, hi, lo)

    element, slot_two = place(z, cell_two_ref[...])
    payload = jnp.concatenate([element + 1.0, ref_two_ref[...]], axis=0)
    send_parts(1, pack(z, payload, low_ref, slot_two))
    for load in loads[2:]:
        load.wait()
    mid_ref[...] = own_part(state, hi, lo)

    def first(i):
        data = chunk_rows(in_one, i)
        fluid = sample(data[:4], hi, lo, *build(data[:4], i))
        drag(0, fluid, data[0:1], data[4:], i)

    take_all(0)
    first(turn(0))
    force_ref[...] = jnp.zeros_like(force_ref)

    def first_step(r, _):
        take(0, r)
        spread(turn(r - 1))
        first(turn(r))
        give(0, r)
        return 0

    lax.fori_loop(1, z.chunks, first_step, 0)
    spread(turn(z.chunks - 1))
    give_all(0)
    mid_ref[...] += force_ref[...].T
    face_wait(0)
    state = mid_ref[...] + widen(partner_faces(0, wide), sel_t_ref[...])
    hi, lo = split2(state)
    wide = send_faces(1, hi, lo)
    mid_ref[...] = own_part(state, hi, lo)
    wait_all(ret_copy, 0)
    unpack(z, ret_in[0], low_ref, slot_one, carry_out)
    carry_out[3:4] = rate
    carry = pltpu.make_async_remote_copy(
        src_ref=carry_out,
        dst_ref=carry_in,
        send_sem=carry_sems.at[0],
        recv_sem=carry_sems.at[1],
        device_id=member(lax.rem(me + n_own - 1, n_own)),
        device_id_type=MESH,
    )
    carry.start()
    wait_all(part_copy, 1)

    def second(i):
        places = chunk_rows(in_two.at[0], i)
        flow[i, 0:3] = sample(places, hi, lo, *build(places, i))

    def second_places(i, _):
        @pl.when(i == z.chunks // 2)
        def _():
            carry.wait()
            pair = jnp.concatenate([carry_out[...], carry_in[...]], axis=1)
            send_parts(2, pack(z, shift(z, pair, cut_ref[0]), low_ref, slot_two))

        second(i)
        return 0

    lax.fori_loop(0, z.chunks, second_places, 0)
    force_ref[...] = jnp.zeros_like(force_ref)
    take_all(2)

    def second_step(r, _):
        @pl.when(r > 0)
        def _():
            take(2, r)

        i = turn(r)
        places = chunk_rows(in_two.at[0], i)
        drag(1, flow[i, 0:3], places[0:1], chunk_rows(in_two.at[1], i), i)
        spread(i)

        @pl.when(r > 0)
        def _():
            give(1, r)

        return 0

    lax.fori_loop(0, z.chunks, second_step, 0)
    give_all(1)
    mid_ref[...] += force_ref[...].T
    face_wait(1)
    joined_ref[...] = partner_faces(1, wide)
    wait_all(ret_copy, 1)
    unpack(z, ret_in[1], low_ref, slot_two, vel_out_ref)


def local(axes, field, neighbours, cell_one, ref_one, cell_two, ref_two, velocity, rate, cut):
    elements, particles = field.shape[1], cell_one.shape[0]
    owners = axes[1] * axes[2]
    z = Sizes(owners, elements, particles)
    selection = face_table()
    own = viscosity * laplace_table() - penalty * np.diag(selection.sum(axis=1))
    own_hi = own.astype(np.float32).astype(b16)
    own_lo = (own - own_hi.astype(np.float64)).astype(np.float32).astype(b16)
    table = np.concatenate([gap_table(), np.eye(8)], axis=1).astype(np.float32)
    vmem = pl.BlockSpec(memory_space=pltpu.VMEM)
    args = [
        field,
        neighbours.T,
        cell_one[None],
        ref_one,
        cell_two[None],
        ref_two,
        velocity,
        rate[None],
        cut,
        jnp.asarray(own_hi),
        jnp.asarray(own_lo),
        jnp.asarray(selection, b16),
        jnp.asarray(selection.T, b16),
        jnp.asarray(table),
    ]
    specs = [vmem] * len(args)
    specs[8] = pl.BlockSpec(memory_space=pltpu.SMEM)
    for index in (0, 9, 10, 11, 12):
        specs[index] = pl.BlockSpec(memory_space=pl.ANY)
    dma = pltpu.SemaphoreType.DMA
    mid, joined, speeds = pl.pallas_call(
        functools.partial(kernel, z, axes),
        out_shape=(
            jax.ShapeDtypeStruct((4 * elements, 512), f32),
            jax.ShapeDtypeStruct((4 * elements, 384), f32),
            jax.ShapeDtypeStruct(velocity.shape, f32),
        ),
        in_specs=specs,
        out_specs=(vmem, vmem, vmem),
        scratch_shapes=[
            pltpu.VMEM(field.shape, f32),
            pltpu.VMEM((512, 512), b16),
            pltpu.VMEM((512, 512), b16),
            pltpu.VMEM((512, 384), b16),
            pltpu.VMEM((384, 512), b16),
            pltpu.VMEM((z.tiles, 8, z.lw), f32),
            pltpu.VMEM((z.tiles, 8, z.lw), f32),
            pltpu.VMEM((2, z.tiles, 4, z.lw), f32),
            pltpu.VMEM((2, z.tiles, 4, z.lw), f32),
            pltpu.VMEM((2, owners, z.rpb, z.lw), f32),
            pltpu.VMEM((2, owners, z.rpb, z.lw), f32),
            pltpu.VMEM((4, particles), f32),
            pltpu.VMEM((4, particles), f32),
            pltpu.VMEM((2, 6, z.edge, 256), f32),
            pltpu.VMEM((2, 6, z.edge, 256), f32),
            pltpu.VMEM((z.chunks, 512, z.chunk), b16),
            pltpu.VMEM((z.chunks, 512, z.chunk), b16),
            pltpu.VMEM((z.chunks, 8, z.chunk), f32),
            pltpu.VMEM((z.chunks, 8, z.chunk), f32),
            pltpu.VMEM((512, 4 * elements), f32),
            pltpu.VMEM((16, particles), f32),
            dma((3, owners)),
            dma((3, owners)),
            dma((2, owners)),
            dma((2, owners)),
            dma((2, 6)),
            dma((2, 6)),
            dma((2,)),
            dma((5,)),
        ],
        compiler_params=pltpu.CompilerParams(
            collective_id=0, has_side_effects=True, vmem_limit_bytes=56 * 1024 * 1024
        ),
    )(*args)
    return pl.pallas_call(
        ending,
        out_shape=(
            jax.ShapeDtypeStruct(field.shape, f32),
            jax.ShapeDtypeStruct(velocity.shape, f32),
        ),
        in_specs=[vmem] * 4,
        out_specs=(vmem, vmem),
        compiler_params=pltpu.CompilerParams(vmem_limit_bytes=56 * 1024 * 1024),
    )(mid, joined, speeds, args[12])


def solution(mesh):
    axes = (mesh.shape["gx"], mesh.shape["gy"], mesh.shape["gz"])
    in_specs = (
        P(None, ("gx", "gy", "gz"), None),
        P(("gx", "gy", "gz"), None),
        P(("gx", "gy", "gz")),
        P(None, ("gx", "gy", "gz")),
        P(("gx", "gy", "gz")),
        P(None, ("gx", "gy", "gz")),
        P(None, ("gx", "gy", "gz")),
        P(("gx", "gy", "gz")),
        P(),
    )
    out_specs = (P(None, ("gx", "gy", "gz"), None), P(None, ("gx", "gy", "gz")))
    return jax.shard_map(
        functools.partial(local, axes), mesh=mesh, in_specs=in_specs, out_specs=out_specs,
        check_vma=False,
    )
```

```python
import functools
import jax
import jax.numpy as jnp
import numpy as np
from jax import lax
from jax.experimental import pallas as pl
from jax.experimental.pallas import tpu as pltpu
from jax.sharding import PartitionSpec as P

EDGE = 4
node_points = -np.cos(np.pi * np.arange(8) / 7.0)
step_time = 0.1
viscosity = 0.002
penalty = 0.25
couplings = (-0.5, -0.5, -0.5, 0.5)
f32 = jnp.float32
b16 = jnp.bfloat16
MESH = pl.DeviceIdType.MESH


def gap_table():
    differences = node_points[:, None] - node_points[None, :] + np.eye(8)
    inverse = 1.0 / differences
    return inverse * (1.0 - np.eye(8))


def laplace_table():
    differences = node_points[:, None] - node_points[None, :] + np.eye(8)
    weights = 1.0 / np.prod(differences, axis=1)
    derivative = weights[None, :] / weights[:, None] / differences
    derivative = derivative * (1.0 - np.eye(8))
    derivative = derivative - np.eye(8) * derivative.sum(axis=1)[:, None]
    second = derivative @ derivative
    identity = np.eye(8)
    operator = np.kron(np.kron(second, identity), identity)
    operator = operator + np.kron(np.kron(identity, second), identity)
    operator = operator + np.kron(np.kron(identity, identity), second)
    return operator.T


def face_table():
    selection = np.zeros((512, 384))
    for side in range(6):
        edge = 0 if side % 2 == 0 else 7
        for row in range(8):
            for col in range(8):
                if side < 2:
                    node = (edge * 8 + row) * 8 + col
                elif side < 4:
                    node = (row * 8 + edge) * 8 + col
                else:
                    node = (row * 8 + col) * 8 + edge
                selection[node, side * 64 + row * 8 + col] = 1.0
    return selection


def mm(a, b):
    return lax.dot_general(a, b, (((1,), (0,)), ((), ())), preferred_element_type=f32)


def nt(a, b):
    return lax.dot_general(a, b, (((1,), (1,)), ((), ())), preferred_element_type=f32)


def split2(x):
    hi = x.astype(b16)
    return hi, (x - hi.astype(f32)).astype(b16)


def split3(x):
    hi = x.astype(b16)
    rest = x - hi.astype(f32)
    mid = rest.astype(b16)
    return hi, mid, (rest - mid.astype(f32)).astype(b16)


def iota(shape, dim):
    return lax.broadcasted_iota(jnp.int32, shape, dim)


def fiota(shape, dim):
    return iota(shape, dim).astype(f32)


def quotient(x, n):
    return jnp.floor((x + 0.5) * (1.0 / n))


def onehot(mask):
    return jnp.where(mask, 1.0, 0.0).astype(f32)


def widen(joined, sel_t):
    rows = joined.shape[0]
    both = mm(jnp.concatenate(split2(joined), axis=0), sel_t)
    return penalty * (both[:rows] + both[rows:])


def ending(mid_ref, joined_ref, vel_ref, sel_t_ref, field_out_ref, vel_out_ref):
    field_out_ref[0] = mid_ref[...] + widen(joined_ref[...], sel_t_ref[...])
    vel_out_ref[...] = vel_ref[...]


class Sizes:
    def __init__(self, owners, elements, particles):
        self.owners, self.elements, self.particles = owners, elements, particles
        self.cap = 2 * particles // owners
        self.lw = min(128, self.cap)
        self.bpo = self.cap // self.lw
        self.tiles = owners * self.bpo
        self.rpb = -(-3 * self.bpo // 8) * 8
        self.opc = max(1, 512 // self.cap)
        self.chunk = self.opc * self.cap
        self.tpc = self.opc * self.bpo
        self.chunks = owners // self.opc
        self.edge = EDGE * EDGE


def place(z, cell):
    number = cell.astype(f32)
    device = quotient(number, z.elements)
    element = number - device * z.elements
    owner = device - quotient(device, z.owners) * z.owners
    marks = onehot(fiota((z.owners, z.particles), 0) == owner)
    parts = z.particles // 128
    rows = parts * z.owners
    stacked = jnp.concatenate([marks[:, c * 128 : (c + 1) * 128] for c in range(parts)], axis=0)
    upper = onehot(iota((128, 128), 0) <= iota((128, 128), 1)).astype(b16)
    inside = mm(stacked.astype(b16), upper)
    totals = jnp.broadcast_to(inside[:, 127:128], (rows, 128)).astype(b16)
    row, col = fiota((rows, rows), 0), fiota((rows, rows), 1)
    row_part, col_part = quotient(row, z.owners), quotient(col, z.owners)
    same = (row - row_part * z.owners) == (col - col_part * z.owners)
    earlier = onehot(same & (col_part < row_part)).astype(b16)
    owner_of = fiota((rows, 128), 0)
    owner_of = owner_of - quotient(owner_of, z.owners) * z.owners
    value = stacked * (inside - 1.0 + mm(earlier, totals) + owner_of * z.cap)
    slot = jnp.concatenate(
        [
            jnp.sum(value[c * z.owners : (c + 1) * z.owners], axis=0, keepdims=True)
            for c in range(parts)
        ],
        axis=1,
    )
    return element, slot


def slot_parts(z, slot):
    high = quotient(slot, z.lw)
    low = slot - high * z.lw
    return high, onehot(fiota((z.lw, z.particles), 0) == low).astype(b16)


def pack(z, payload, slot):
    fields = payload.shape[0]
    high, low = slot_parts(z, slot)
    two = jnp.concatenate([part.astype(f32) for part in split2(payload)], axis=0)
    spread = jnp.concatenate(
        [jnp.where(high == float(i), two, 0.0) for i in range(z.tiles)], axis=0
    ).astype(b16)
    moved = nt(spread, low).reshape(z.tiles, 2 * fields, z.lw)
    return moved[:, :fields] + moved[:, fields:]


def unpack(z, block, slot):
    high, low = slot_parts(z, slot)
    rows = z.owners * z.rpb
    flat = block.reshape(rows, z.lw)
    got = mm(jnp.concatenate(split2(flat), axis=0), low)
    got = got[:rows] + got[rows:]
    row = fiota((z.rpb, z.particles), 0)
    key = high - (row - quotient(row, z.bpo) * z.bpo)
    total = jnp.zeros((z.rpb, z.particles), f32)
    for o in range(z.owners):
        total = total + jnp.where(
            key == float(o * z.bpo), got[o * z.rpb : (o + 1) * z.rpb], 0.0
        )
    return jnp.concatenate(
        [
            jnp.sum(total[v * z.bpo : (v + 1) * z.bpo], axis=0, keepdims=True)
            for v in range(3)
        ],
        axis=0,
    )


def shift(z, pair, cut):
    bit = 1 << (z.particles - 1).bit_length() - 1
    while bit >= 1:
        flag = jnp.full(pair.shape, (cut // bit) % 2, jnp.int32) == 1
        if bit >= 128:
            width = z.particles + bit
            pair = jnp.where(flag[:, :width], pair[:, bit : bit + width], pair[:, :width])
        else:
            pair = jnp.where(flag, pltpu.roll(pair, pair.shape[1] - bit, 1), pair)
        bit //= 2
    return pair[:, : z.particles]


def lagrange(x, table):
    result = None
    for m in range(8):
        factor = (x - float(np.float32(node_points[m]))) * table[:, m : m + 1]
        factor = factor + table[:, 8 + m : 9 + m]
        result = factor if result is None else result * factor
    return result


def basis(coords, table):
    first, second, third = [lagrange(coords[d : d + 1], table) for d in range(3)]
    plane = jnp.concatenate([second[b : b + 1] * third for b in range(8)], axis=0)
    return jnp.concatenate([first[a : a + 1] * plane for a in range(8)], axis=0)


def kernel(
    z, axes, field_hbm, nbr_t_ref, cell_one_ref, ref_one_ref, cell_two_ref, ref_two_ref,
    vel_ref, rate_ref, cut_ref, own_hi_hbm, own_lo_hbm, sel_hbm, sel_t_hbm, table_ref,
    mid_ref, joined_ref, vel_out_ref,
    field_ref, own_hi_ref, own_lo_ref, sel_ref, sel_t_ref,
    out_one, in_one, out_two, in_two, ret_out, ret_in, carry_out, carry_in, face_out, face_in,
    w_ref, src, force_ref,
    a2a_send, a2a_recv, ret_send, ret_recv, face_send, face_recv, carry_sems, load_sems,
):
    loads = [
        pltpu.make_async_copy(here, there, load_sems.at[index])
        for index, (here, there) in enumerate(
            [
                (field_hbm, field_ref),
                (sel_hbm, sel_ref),
                (own_hi_hbm, own_hi_ref),
                (own_lo_hbm, own_lo_ref),
                (sel_t_hbm, sel_t_ref),
            ]
        )
    ]
    for load in loads:
        load.start()

    count_x, count_y, count_z = axes
    ix, iy, iz = lax.axis_index("gx"), lax.axis_index("gy"), lax.axis_index("gz")
    me = iy * count_z + iz
    elements, n_own = z.elements, z.owners
    base = ((ix * n_own + me) * elements).astype(jnp.int32)

    def member(index):
        return (ix, index // count_z, index % count_z)

    def peer(r):
        return lax.rem(me + r, n_own)

    barrier = pltpu.get_barrier_semaphore()

    def greet(r, _):
        pl.semaphore_signal(barrier, inc=1, device_id=member(peer(r)), device_id_type=MESH)
        return 0

    lax.fori_loop(1, n_own, greet, 0)
    up_x = (lax.rem(ix + 1, count_x), iy, iz)
    down_x = (lax.rem(ix + count_x - 1, count_x), iy, iz)
    for device in (up_x, down_x):
        pl.semaphore_signal(barrier, inc=1, device_id=device, device_id_type=MESH)

    def outgoing(stage):
        return (out_one, in_one) if stage == 0 else (out_two.at[stage - 1], in_two.at[stage - 1])

    def part_copy(stage, r):
        to = peer(r)
        source, target = outgoing(stage)
        return pltpu.make_async_remote_copy(
            src_ref=source.at[pl.ds(to * z.bpo, z.bpo)],
            dst_ref=target.at[pl.ds(me * z.bpo, z.bpo)],
            send_sem=a2a_send.at[stage, r],
            recv_sem=a2a_recv.at[stage, r],
            device_id=member(to),
            device_id_type=MESH,
        )

    def ret_copy(stage, r):
        to = peer(r)
        return pltpu.make_async_remote_copy(
            src_ref=ret_out.at[stage, to],
            dst_ref=ret_in.at[stage, me],
            send_sem=ret_send.at[stage, r],
            recv_sem=ret_recv.at[stage, r],
            device_id=member(to),
            device_id_type=MESH,
        )

    def start_all(make, stage):
        def body(r, _):
            make(stage, r).start()
            return 0

        lax.fori_loop(1, n_own, body, 0)

    def wait_all(make, stage):
        def body(r, _):
            make(stage, r).wait()
            return 0

        lax.fori_loop(1, n_own, body, 0)

    def send_parts(stage, packed):
        source, target = outgoing(stage)
        source[...] = packed
        own = pl.ds(me * z.bpo, z.bpo)
        target[own] = source[own]
        start_all(part_copy, stage)

    def take(stage, r):
        if z.opc == 1:
            part_copy(stage, r).wait()

    def give(stage, r):
        if z.opc == 1:
            ret_copy(stage, n_own - r).start()

    def take_all(stage):
        if z.opc > 1:
            wait_all(part_copy, stage)

    def give_all(stage):
        ret_in[stage, me] = ret_out[stage, me]
        if z.opc > 1:
            start_all(ret_copy, stage)

    def turn(r):
        return lax.rem(me + n_own - r, n_own) if z.opc == 1 else r

    face_devices = [
        down_x,
        up_x,
        (ix, lax.rem(iy + count_y - 1, count_y), iz),
        (ix, lax.rem(iy + 1, count_y), iz),
        (ix, iy, lax.rem(iz + count_z - 1, count_z)),
        (ix, iy, lax.rem(iz + 1, count_z)),
    ]

    def face_copy(stage, side):
        return pltpu.make_async_remote_copy(
            src_ref=face_out.at[stage, side],
            dst_ref=face_in.at[stage, side ^ 1],
            send_sem=face_send.at[stage, side],
            recv_sem=face_recv.at[stage, side ^ 1],
            device_id=face_devices[side],
            device_id_type=MESH,
        )

    def face_wait(stage):
        for side in range(6):
            face_copy(stage, side).wait_send()
        for side in range(6):
            pltpu.make_async_remote_copy(
                src_ref=face_out.at[stage, side ^ 1],
                dst_ref=face_in.at[stage, side],
                send_sem=face_send.at[stage, side ^ 1],
                recv_sem=face_recv.at[stage, side],
                device_id=face_devices[side],
                device_id_type=MESH,
            ).wait_recv()

    table = table_ref[...]

    rate = rate_ref[...]
    element, slot_one = place(z, cell_one_ref[...])
    packed = pack(
        z, jnp.concatenate([element + 1.0, ref_one_ref[...], vel_ref[...], rate], axis=0), slot_one
    )
    pl.semaphore_wait(barrier, n_own - 1 + 2)
    send_parts(0, packed)

    square = (elements, elements)
    rows = nbr_t_ref[...].astype(f32)
    columns = jnp.concatenate([rows, rows[:2]], axis=0).T
    base = base.astype(f32)
    compacts, partners = [], []
    for side in range(6):
        col = columns[:, side : side + 1]
        row = rows[side : side + 1, :]
        col_out = (col < base) | (col >= base + elements)
        row_out = (row < base) | (row >= base + elements)
        before = jnp.where(col_out & (iota(square, 0) < iota(square, 1)), 1.0, 0.0)
        before = jnp.sum(before, axis=0, keepdims=True)
        compact = onehot((fiota((z.edge, elements), 0) == before) & row_out).astype(b16)
        compacts.append(jnp.concatenate([compact, compact], axis=1))
        here = onehot(fiota(square, 1) == col - base).astype(b16)
        lower = jnp.where(row_out & (row >= 0) & (row < col), 1.0, 0.0)
        rank = jnp.sum(lower, axis=1, keepdims=True)
        far = onehot((fiota((elements, z.edge), 1) == rank) & col_out & (col >= 0)).astype(b16)
        partners.append(jnp.concatenate([here, here, far, far], axis=1))

    def split_state(state):
        return split2(state.reshape(4 * elements, 512))

    def send_faces(stage, hi, lo):
        both = mm(jnp.concatenate([hi, lo], axis=0), sel_ref[...])
        faces = both[: 4 * elements] + both[4 * elements :]
        wide = []
        for side in range(6):
            lanes = jnp.concatenate(
                [
                    faces[k * elements : (k + 1) * elements, side * 64 : (side + 1) * 64]
                    for k in range(4)
                ],
                axis=1,
            )
            pair = jnp.concatenate(split2(lanes), axis=0)
            wide.append(pair)
            face_out[stage, side] = mm(compacts[side], pair)
            face_copy(stage, side).start()
        return wide

    def own_part(state, hi, lo):
        both = mm(jnp.concatenate([hi, lo], axis=0), own_hi_ref[...])
        rows = 4 * elements
        return state + both[:rows] + both[rows:] + mm(hi, own_lo_ref[...])

    def partner_faces(stage, wide):
        got = []
        for side in range(6):
            far = jnp.concatenate(split2(face_in[stage, side]), axis=0)
            got.append(mm(partners[side], jnp.concatenate([wide[side ^ 1], far], axis=0)))
        return jnp.concatenate(
            [
                jnp.concatenate([got[side][:, k * 64 : (k + 1) * 64] for side in range(6)], axis=1)
                for k in range(4)
            ],
            axis=0,
        )

    def chunk_rows(ref, i):
        piece = ref[pl.ds(i * z.tpc, z.tpc)]
        return jnp.concatenate([piece[t] for t in range(z.tpc)], axis=1)

    def sample(places, hi, lo, i):
        w_up, w_down = split2(basis(places[1:4], table))
        w_ref[i, 0:512] = w_up
        w_ref[i, 512:1024] = w_down
        rows = 3 * elements
        both = mm(jnp.concatenate([hi[:rows], lo[:rows]], axis=0), w_up)
        values = both[:rows] + both[rows:] + mm(hi[:rows], w_down)
        pick = fiota((elements, z.chunk), 0) == places[0:1] - 1.0
        return jnp.concatenate(
            [
                jnp.sum(
                    jnp.where(pick, values[k * elements : (k + 1) * elements], 0.0),
                    axis=0,
                    keepdims=True,
                )
                for k in range(3)
            ],
            axis=0,
        )

    def drag(stage, fluid, place_row, dynamic, i):
        speeds, rates = dynamic[:3], dynamic[3:4]
        offset = fluid - speeds
        accel = rates * offset
        heat = rates * jnp.sum(offset * offset, axis=0, keepdims=True)
        fresh = speeds + step_time * accel
        src[i] = jnp.concatenate(
            [couplings[0] * accel, couplings[3] * heat, place_row, fresh], axis=0
        )
        for j in range(z.opc):
            rows = []
            for v in range(3):
                for b in range(z.bpo):
                    at = j * z.cap + b * z.lw
                    rows.append(fresh[v : v + 1, at : at + z.lw])
            if z.rpb > 3 * z.bpo:
                rows.append(jnp.zeros((z.rpb - 3 * z.bpo, z.lw), f32))
            ret_out[stage, i * z.opc + j] = jnp.concatenate(rows, axis=0)

    def spread(i):
        data = src[i]
        pick = fiota((elements, z.chunk), 0) == data[4:5] - 1.0
        loads = jnp.concatenate([jnp.where(pick, data[k : k + 1], 0.0) for k in range(4)], axis=0)
        hi, lo = split2(loads)
        both = nt(w_ref[i], hi)
        return both[:512] + both[512:] + nt(w_ref[i, 0:512], lo)

    for load in loads[:2]:
        load.wait()
    state = field_ref[...].reshape(4 * elements, 512)
    hi, lo = split2(state)
    wide = send_faces(0, hi, lo)

    element, slot_two = place(z, cell_two_ref[...])
    send_parts(
        1, pack(z, jnp.concatenate([element + 1.0, ref_two_ref[...]], axis=0), slot_two)
    )
    for load in loads[2:]:
        load.wait()
    mid_ref[...] = own_part(state, hi, lo)

    def first(i):
        data = chunk_rows(in_one, i)
        drag(0, sample(data[:4], hi, lo, i), data[0:1], data[4:], i)

    take_all(0)
    first(turn(0))
    force_ref[...] = jnp.zeros_like(force_ref)

    def first_step(r, _):
        take(0, r)
        force_ref[...] += spread(turn(r - 1))
        first(turn(r))
        give(0, r)
        return 0

    lax.fori_loop(1, z.chunks, first_step, 0)
    give_all(0)
    force = force_ref[...] + spread(turn(z.chunks - 1))
    mid_ref[...] += force.T
    face_wait(0)
    state = mid_ref[...] + widen(partner_faces(0, wide), sel_t_ref[...])
    hi, lo = split2(state)
    wide = send_faces(1, hi, lo)
    mid_ref[...] = own_part(state, hi, lo)
    wait_all(ret_copy, 0)
    carry_out[...] = jnp.concatenate([unpack(z, ret_in[0], slot_one), rate], axis=0)
    carry = pltpu.make_async_remote_copy(
        src_ref=carry_out,
        dst_ref=carry_in,
        send_sem=carry_sems.at[0],
        recv_sem=carry_sems.at[1],
        device_id=member(lax.rem(me + n_own - 1, n_own)),
        device_id_type=MESH,
    )
    carry.start()
    wait_all(part_copy, 1)

    def second(i):
        places = chunk_rows(in_two.at[0], i)
        src[i, 0:3] = sample(places, hi, lo, i)

    half = z.chunks // 2
    for i in range(half):
        second(i)
    carry.wait()
    moved = shift(z, jnp.concatenate([carry_out[...], carry_in[...]], axis=1), cut_ref[0])
    send_parts(2, pack(z, moved, slot_two))
    for i in range(half, z.chunks):
        second(i)
    force_ref[...] = jnp.zeros_like(force_ref)
    take_all(2)

    def finish(i):
        places = chunk_rows(in_two.at[0], i)
        drag(1, src[i, 0:3], places[0:1], chunk_rows(in_two.at[1], i), i)

    finish(turn(0))

    def second_step(r, _):
        take(2, r)
        finish(turn(r))
        force_ref[...] += spread(turn(r - 1))
        give(1, r)
        return 0

    lax.fori_loop(1, z.chunks, second_step, 0)
    give_all(1)
    force = force_ref[...] + spread(turn(z.chunks - 1))
    mid_ref[...] += force.T
    face_wait(1)
    joined_ref[...] = partner_faces(1, wide)
    wait_all(ret_copy, 1)
    vel_out_ref[...] = unpack(z, ret_in[1], slot_two)


def local(axes, field, neighbours, cell_one, ref_one, cell_two, ref_two, velocity, rate, cut):
    elements, particles = field.shape[1], cell_one.shape[0]
    owners = axes[1] * axes[2]
    z = Sizes(owners, elements, particles)
    selection = face_table()
    own = viscosity * laplace_table() - penalty * np.diag(selection.sum(axis=1))
    own_hi = own.astype(np.float32).astype(b16)
    own_lo = (own - own_hi.astype(np.float64)).astype(np.float32).astype(b16)
    table = np.concatenate([gap_table(), np.eye(8)], axis=1).astype(np.float32)
    vmem = pl.BlockSpec(memory_space=pltpu.VMEM)
    args = [
        field,
        neighbours.T,
        cell_one[None],
        ref_one,
        cell_two[None],
        ref_two,
        velocity,
        rate[None],
        cut,
        jnp.asarray(own_hi),
        jnp.asarray(own_lo),
        jnp.asarray(selection, b16),
        jnp.asarray(selection.T, b16),
        jnp.asarray(table),
    ]
    specs = [vmem] * len(args)
    specs[8] = pl.BlockSpec(memory_space=pltpu.SMEM)
    for index in (0, 9, 10, 11, 12):
        specs[index] = pl.BlockSpec(memory_space=pl.ANY)
    dma = pltpu.SemaphoreType.DMA
    mid, joined, speeds = pl.pallas_call(
        functools.partial(kernel, z, axes),
        out_shape=(
            jax.ShapeDtypeStruct((4 * elements, 512), f32),
            jax.ShapeDtypeStruct((4 * elements, 384), f32),
            jax.ShapeDtypeStruct(velocity.shape, f32),
        ),
        in_specs=specs,
        out_specs=(vmem, vmem, vmem),
        scratch_shapes=[
            pltpu.VMEM(field.shape, f32),
            pltpu.VMEM((512, 512), b16),
            pltpu.VMEM((512, 512), b16),
            pltpu.VMEM((512, 384), b16),
            pltpu.VMEM((384, 512), b16),
            pltpu.VMEM((z.tiles, 8, z.lw), f32),
            pltpu.VMEM((z.tiles, 8, z.lw), f32),
            pltpu.VMEM((2, z.tiles, 4, z.lw), f32),
            pltpu.VMEM((2, z.tiles, 4, z.lw), f32),
            pltpu.VMEM((2, owners, z.rpb, z.lw), f32),
            pltpu.VMEM((2, owners, z.rpb, z.lw), f32),
            pltpu.VMEM((4, particles), f32),
            pltpu.VMEM((4, particles), f32),
            pltpu.VMEM((2, 6, z.edge, 256), f32),
            pltpu.VMEM((2, 6, z.edge, 256), f32),
            pltpu.VMEM((z.chunks, 1024, z.chunk), b16),
            pltpu.VMEM((z.chunks, 8, z.chunk), f32),
            pltpu.VMEM((512, 4 * elements), f32),
            dma((3, owners)),
            dma((3, owners)),
            dma((2, owners)),
            dma((2, owners)),
            dma((2, 6)),
            dma((2, 6)),
            dma((2,)),
            dma((5,)),
        ],
        compiler_params=pltpu.CompilerParams(
            collective_id=0, has_side_effects=True, vmem_limit_bytes=56 * 1024 * 1024
        ),
    )(*args)
    whole = pl.BlockSpec(velocity.shape, lambda k: (0, 0))
    return pl.pallas_call(
        ending,
        grid=(4,),
        out_shape=(
            jax.ShapeDtypeStruct(field.shape, f32),
            jax.ShapeDtypeStruct(velocity.shape, f32),
        ),
        in_specs=[
            pl.BlockSpec((elements, 512), lambda k: (k, 0)),
            pl.BlockSpec((elements, 384), lambda k: (k, 0)),
            whole,
            pl.BlockSpec((384, 512), lambda k: (0, 0)),
        ],
        out_specs=(pl.BlockSpec((1, elements, 512), lambda k: (k, 0, 0)), whole),
        compiler_params=pltpu.CompilerParams(vmem_limit_bytes=56 * 1024 * 1024),
    )(mid, joined, speeds, args[12])


def solution(mesh):
    axes = (mesh.shape["gx"], mesh.shape["gy"], mesh.shape["gz"])
    in_specs = (
        P(None, ("gx", "gy", "gz"), None),
        P(("gx", "gy", "gz"), None),
        P(("gx", "gy", "gz")),
        P(None, ("gx", "gy", "gz")),
        P(("gx", "gy", "gz")),
        P(None, ("gx", "gy", "gz")),
        P(None, ("gx", "gy", "gz")),
        P(("gx", "gy", "gz")),
        P(),
    )
    out_specs = (P(None, ("gx", "gy", "gz"), None), P(None, ("gx", "gy", "gz")))
    return jax.shard_map(
        functools.partial(local, axes), mesh=mesh, in_specs=in_specs, out_specs=out_specs,
        check_vma=False,
    )
```
